32 devices in a mesh: seq: 8 (over y, x, core), col: 4 (over z).
Axes of the slice: x: 2, y: 2, z: 4, core: 2. Of those that a mesh axis runs over, the one named last changes fastest.
Arguments:
- bases: int32 [2, 8192, 128], P(None, 'seq'), may hold values from 0 to 3
- stem_weight: bfloat16 [512, 1536], P(None, 'col'), may hold values from -0.5 to 0.5
- conv_weight: bfloat16 [5, 1536, 1536], P(None, 'col'), may hold values from -0.0625 to 0.0625
- conv_bias: float32 [1536], P('col'), may hold values from -3 to 3
- pair_proj: bfloat16 [1536, 256], P('col'), may hold values from -0.625 to 0.625
- pair_weight: bfloat16 [128, 128], replicated, may hold values from -0.5 to 0.5
- pair_cotangent: bfloat16 [2, 512, 512, 128], P(None, 'seq', 'col'), may hold values from -6 to 6
- pair_mask: int32 [512, 512], P('seq', 'col'), may hold values 0 or 1
Outputs:
- token_grad: bfloat16 [2, 8192, 1536], P(None, 'seq', 'col')
- conv_weight_grad: bfloat16 [5, 1536, 1536], P(None, 'col')
- pair_weight_grad: float32 [128, 128], replicated
The draws below stay inside these ranges and needn't reach their ends.
All inputs are finite; a program needn't handle non-finite values. No bound on the sum of `pair_mask` on one device may be relied on, other than what follows from the above.
Results may differ from the reference program's by a relative error of at most 0.012.
Values may be sent and summed in bfloat16 or wider, within the bound.
No kernel may reach another device: no remote copies, remote signals or barrier semaphores. Data moves between devices by JAX's collectives and lax.ppermute only.
A program may use at most 128 MiB of HBM per device.

```python
import jax
import jax.numpy as jnp
from jax import lax

C = 1536
CP = 128
KW = 5
BP = 128
POOL = 16
L = 8192
SEQS = 2
P_SIZE = 512


def with_ends(values, own_key, low, high):
    longest = values.shape.index(max(values.shape))
    spots = []
    for shift in (0, 1):
        where = [jax.random.randint(jax.random.fold_in(own_key, axis), (), 0, length) for axis, length in enumerate(values.shape)]
        where[longest] = (where[longest] + shift) % values.shape[longest]
        spots.append(tuple(where))
    return values.at[spots[0]].set(low).at[spots[1]].set(high)


def block_scale(stream_key, extent, cuts, smallest, top_value):
    loudness = 1.0
    for dim, parts in cuts:
        heights = jax.random.uniform(jax.random.fold_in(jax.random.fold_in(stream_key, 6), dim), (parts,), jnp.float32, smallest / len(cuts), top_value / len(cuts))
        loudness = loudness * jnp.repeat(jnp.exp(heights), extent[dim] // parts).reshape((-1,) + (1,) * (len(extent) - 1 - dim))
    return loudness


def scatter_about(stream_key, extent, spread, bound, cuts=(), kind=jnp.bfloat16):
    result = jax.random.normal(stream_key, extent, jnp.float32) * spread
    if len(cuts) > 0:
        result = block_scale(stream_key, extent, cuts, -0.22, 0.18) * result
    return jnp.clip(result, min=-bound, max=bound).astype(kind)


def setup_inputs(seed: int = 0) -> dict:
    streams_of = jax.random.split(jax.random.key(seed), 9)
    return {
        "bases": with_ends(jax.random.randint(streams_of[0], (SEQS, L, BP), 0, 4), jax.random.fold_in(streams_of[0], 1), 0, 3).astype(jnp.int32),
        "stem_weight": scatter_about(streams_of[1], (4 * BP, C), BP ** -0.5, 0.5, ((1, 4),)),
        "conv_weight": scatter_about(streams_of[2], (KW, C, C), (KW * C) ** -0.5, 0.0625, ((1, 4),)),
        "conv_bias": scatter_about(streams_of[3], (C,), 0.5, 3.0, ((0, 4),), jnp.float32),
        "pair_proj": scatter_about(streams_of[4], (C, 2 * CP), (C // 16) ** -0.5, 0.625, ((0, 4),)),
        "pair_weight": scatter_about(streams_of[5], (CP, CP), CP ** -0.5, 0.5),
        "pair_cotangent": scatter_about(streams_of[6], (SEQS, P_SIZE, P_SIZE, CP), 1.0, 6.0, ((1, 8), (2, 4))),
        "pair_mask": with_ends((jax.random.randint(streams_of[7], (P_SIZE, P_SIZE), 0, 4) < 3).astype(jnp.int32), jax.random.fold_in(streams_of[7], 1), 0, 1),
    }


def gelu_slope(values):
    return jax.vjp(jax.nn.gelu, values)[1](jnp.ones_like(values))[0]

def reference(bases, stem_weight, conv_weight, conv_bias, pair_proj, pair_weight, pair_cotangent, pair_mask):
    levels = jnp.arange(4, dtype=jnp.int32)
    onehot = (bases[..., None] == levels).astype(jnp.float32).reshape(SEQS, L, 4 * BP)
    embedded = jnp.einsum('bik,kc->bic', onehot, stem_weight.astype(jnp.float32)).astype(jnp.bfloat16)
    weights = conv_weight.astype(jnp.float32)
    padded = jnp.pad(embedded.astype(jnp.float32), ((0, 0), (2, 2), (0, 0)))
    conv_out = conv_bias[None, None, :]
    for tap in range(KW):
        conv_out = conv_out + jnp.einsum('bic,oc->bio', padded[:, tap:tap + L], weights[tap])
    features = (embedded.astype(jnp.float32) + jax.nn.gelu(conv_out)).astype(jnp.bfloat16)
    pooled = features.astype(jnp.float32).reshape(SEQS, P_SIZE, POOL, C).mean(2)
    proj_f = pair_proj.astype(jnp.float32)
    projected = jnp.einsum('bmc,cp->bmp', pooled, proj_f, precision=lax.Precision.HIGHEST)
    row_feat = projected[..., :CP]
    col_feat = projected[..., CP:]
    pre_act = row_feat[:, :, None, :] + col_feat[:, None, :, :]
    activ = jax.nn.gelu(pre_act).astype(jnp.bfloat16)
    masked = pair_cotangent * pair_mask[None, :, :, None].astype(jnp.bfloat16)
    masked_f = masked.astype(jnp.float32)
    pair_weight_grad = jnp.einsum('bmnp,bmnq->pq', activ.astype(jnp.float32), masked_f)
    back = jnp.einsum('bmnq,pq->bmnp', masked_f, pair_weight.astype(jnp.float32))
    pre_grad = back * gelu_slope(pre_act)
    row_grad = pre_grad.sum(2)
    col_grad = pre_grad.sum(1)
    both_grad = jnp.concatenate([row_grad, col_grad], axis=-1)
    pooled_grad = jnp.einsum('bmp,cp->bmc', both_grad, proj_f, precision=lax.Precision.HIGHEST)
    feat_grad = jnp.repeat(pooled_grad, POOL, axis=1) / POOL
    conv_grad = (feat_grad * gelu_slope(conv_out)).astype(jnp.bfloat16)
    grad_f = conv_grad.astype(jnp.float32)
    conv_weight_grad = jnp.stack([jnp.einsum('bio,bic->oc', grad_f, padded[:, tap:tap + L]) for tap in range(KW)]).astype(jnp.bfloat16)
    grad_pad = jnp.pad(grad_f, ((0, 0), (2, 2), (0, 0)))
    input_grad = jnp.zeros((SEQS, L, C), jnp.float32)
    for tap in range(KW):
        input_grad = input_grad + jnp.einsum('bjo,oc->bjc', grad_pad[:, 4 - tap:4 - tap + L], weights[tap])
    token_grad = (feat_grad + input_grad).astype(jnp.bfloat16)
    return (token_grad, conv_weight_grad, pair_weight_grad)
```

```python
import functools

import jax
import jax.numpy as jnp
from jax import lax
from jax.experimental import pallas as pl
from jax.experimental.pallas import tpu as pltpu
from jax.sharding import PartitionSpec as P

BF, F32 = jnp.bfloat16, jnp.float32
EDGE = 16
WIN = 24
ROOT = 0.7978845608028654
CUBE = 0.044715


def gelu_parts(x):
    sq = x * x
    th = jnp.tanh(x * (ROOT + (ROOT * CUBE) * sq))
    half = 0.5 + 0.5 * th
    act = x * half
    return act, half + act * (1.0 - th) * (ROOT + (3.0 * ROOT * CUBE) * sq)


def dot_nn(a, b):
    return lax.dot_general(a, b, (((1,), (0,)), ((), ())), preferred_element_type=F32)


def dot_nt(a, b):
    return lax.dot_general(a, b, (((1,), (1,)), ((), ())), preferred_element_type=F32)


def dot_tn(a, b):
    return lax.dot_general(a, b, (((0,), (0,)), ((), ())), preferred_element_type=F32)


def dot_split(a, b):
    hi = a.astype(BF)
    rest = a - hi.astype(F32)
    mid = rest.astype(BF)
    low = (rest - mid.astype(F32)).astype(BF)
    return dot_nn(hi, b) + dot_nn(mid, b) + dot_nn(low, b)


def xor_pairs(count, step):
    return [(i, i ^ step) for i in range(count)]


def sum_over(x, axis, first=0):
    for step in powers(lax.axis_size(axis))[first:]:
        x = swap_add(x, axis, step)
    return x


def after(x, *earlier):
    return lax.optimization_barrier((x,) + earlier)[0]


def swap_add(x, axis, step):
    return x + lax.ppermute(x, axis, xor_pairs(lax.axis_size(axis), step))


def powers(count):
    steps = [1]
    while 2 * steps[-1] < count:
        steps.append(2 * steps[-1])
    return steps


def window_onehot(win, first, rows, taps, levels=4):
    parts = []
    for tap in range(taps):
        own = win[first + tap : first + tap + rows]
        for level in range(levels):
            parts.append(jnp.where(own == level + 1, 1.0, 0.0).astype(BF))
    return jnp.concatenate(parts, axis=1)


def spread(pg, pool):
    groups, chan = pg.shape
    return jnp.broadcast_to(pg[:, None, :], (groups, pool, chan)).reshape(groups * pool, chan)


def params(**kw):
    return pltpu.CompilerParams(vmem_limit_bytes=56 * 1024 * 1024, **kw)


def fold_kernel(place, own, mine, other, w, stem_out, own_out, m_out, *, cols):
    bits, chan = own.shape
    half = bits // 2
    per = bits // 4

    @pl.when(pl.program_id(0) == 0)
    def _():
        b, c = place[0], place[1]

        def pick(width, base):
            dst = lax.broadcasted_iota(jnp.int32, (bits, width), 0)
            src = 4 * (dst % per) + dst // per
            at = lax.broadcasted_iota(jnp.int32, (bits, width), 1) + base
            return jnp.where(src == at, 1.0, 0.0).astype(BF)

        own_p = dot_nn(pick(bits, 0), own[...]).astype(BF)
        own_out[...] = own_p
        pick_mine, pick_other = pick(half, half * c), pick(half, half * (1 - c))
        for j in range(cols):
            k = lax.rem(j - b + cols, cols)
            at = jnp.maximum(k - 1, 0)
            got = dot_nn(pick_mine, mine[at]) + dot_nn(pick_other, other[at])
            stem_out[:, j * chan : (j + 1) * chan] = jnp.where(k == 0, own_p, got.astype(BF))

    m_out[...] = dot_nt(stem_out[...], w[0]).astype(BF)


def fold(place, own, mine, other, weight):
    taps, chan, full = weight.shape
    bits = own.shape[0]
    cols = full // chan
    whole = lambda t, p: (0, 0)
    whole3 = lambda t, p: (0, 0, 0)
    return pl.pallas_call(
        functools.partial(fold_kernel, cols=cols),
        grid_spec=pltpu.PrefetchScalarGridSpec(
            num_scalar_prefetch=1,
            grid=(taps,),
            in_specs=[
                pl.BlockSpec(own.shape, whole),
                pl.BlockSpec(mine.shape, whole3),
                pl.BlockSpec(other.shape, whole3),
                pl.BlockSpec((1, chan, full), lambda t, p: (t, 0, 0)),
            ],
            out_specs=[
                pl.BlockSpec((bits, full), whole),
                pl.BlockSpec((bits, chan), whole),
                pl.BlockSpec((bits, chan), lambda t, p: (t, 0)),
            ],
        ),
        out_shape=[
            jax.ShapeDtypeStruct((bits, full), BF),
            jax.ShapeDtypeStruct((bits, chan), BF),
            jax.ShapeDtypeStruct((taps * bits, chan), BF),
        ],
        compiler_params=params(),
        cost_estimate=pl.CostEstimate(
            flops=2 * taps * bits * chan * full, bytes_accessed=8_000_000, transcendentals=0
        ),
        name="fold",
    )(place, own, mine, other, weight)


def forward_kernel(bases, m, stem, bias, proj, slope_out, proj_out, *, tiles, taps, pool):
    rows = slope_out.shape[1] // tiles
    bits = stem.shape[0]
    mid = taps // 2
    pooled = []
    for i in range(tiles):
        win = bases[0, i * rows : i * rows + rows + EDGE, :]
        x = window_onehot(win, WIN - EDGE - mid, rows, taps)
        conv = dot_nn(x, m[...]) + bias[...]
        embedded = dot_nn(x[:, mid * bits : (mid + 1) * bits], stem[...]).astype(BF)
        act, slope = gelu_parts(conv)
        slope_out[0, i * rows : (i + 1) * rows, :] = slope.astype(BF)
        feats = (embedded.astype(F32) + act).astype(BF).astype(F32)
        pooled.append(feats.reshape(rows // pool, pool, feats.shape[1]).sum(1))
    pooled = jnp.concatenate(pooled, axis=0)
    inner = EDGE // pool
    pooled = pooled[inner : inner + proj_out.shape[1]] * (1.0 / pool)
    proj_out[0] = dot_split(pooled, proj[...])


def row_tiles(rows):
    for tiles in range(1, rows + 1):
        if rows % (tiles * 16) == 0 and rows // tiles <= 352:
            return tiles
    return 1


def forward(bases, m, stem, bias, proj, taps, pool):
    batch, ext_rows, width = bases.shape
    rows = ext_rows - 2 * (WIN - EDGE)
    chan = stem.shape[1]
    pairs = (rows - 2 * EDGE) // pool
    two = lambda s: (0, 0)
    return pl.pallas_call(
        functools.partial(forward_kernel, tiles=row_tiles(rows), taps=taps, pool=pool),
        grid=(batch,),
        in_specs=[
            pl.BlockSpec((1, ext_rows, width), lambda s: (s, 0, 0)),
            pl.BlockSpec(m.shape, two),
            pl.BlockSpec(stem.shape, two),
            pl.BlockSpec(bias.shape, two),
            pl.BlockSpec(proj.shape, two),
        ],
        out_specs=[
            pl.BlockSpec((1, rows, chan), lambda s: (s, 0, 0)),
            pl.BlockSpec((1, pairs, proj.shape[1]), lambda s: (s, 0, 0)),
        ],
        out_shape=[
            jax.ShapeDtypeStruct((batch, rows, chan), BF),
            jax.ShapeDtypeStruct((batch, pairs, proj.shape[1]), F32),
        ],
        compiler_params=params(),
        cost_estimate=pl.CostEstimate(
            flops=2 * batch * rows * m.shape[0] * chan, bytes_accessed=6_000_000, transcendentals=0
        ),
        name="forward",
    )(bases, m, stem, bias, proj)


def others_kernel(place, bases, bias, *refs, tiles, taps, pieces):
    part = refs[:pieces]
    out = refs[pieces]
    m_all, sems = refs[pieces + 1 :]
    blocks, slab, chan = part[0].shape
    rows = out.shape[1] // tiles
    mid = taps // 2

    copies = []
    for r in range(pieces):
        a = place[2] ^ r
        for q in range(blocks):
            copies.append(
                pltpu.make_async_copy(
                    part[r].at[q],
                    m_all.at[pl.ds(pl.multiple_of(a * slab, 16), slab), q * chan : (q + 1) * chan],
                    sems.at[r, q],
                )
            )
    for copy in copies:
        copy.start()
    for copy in copies:
        copy.wait()

    lines = []
    for q in range(blocks):
        three = bias[q + 1, -16:, :].astype(F32)
        lines.append(three[0:1] + three[1:2] + three[2:3])
    line = jnp.concatenate(lines, axis=1)
    for i in range(tiles):
        win = bases[0, i * rows : i * rows + rows + EDGE, :]
        x = window_onehot(win, WIN - EDGE - mid, rows, taps)
        conv = dot_nn(x, m_all[...]) + line
        out[0, i * rows : (i + 1) * rows, :] = gelu_parts(conv)[1].astype(BF)


def others(place, bases, bias, part, taps, which):
    batch, ext_rows, width = bases.shape
    rows = ext_rows - 2 * (WIN - EDGE)
    blocks, slab, chan = part[0].shape
    count = len(part)
    return pl.pallas_call(
        functools.partial(
            others_kernel, tiles=row_tiles(rows), taps=taps, pieces=count
        ),
        grid_spec=pltpu.PrefetchScalarGridSpec(
            num_scalar_prefetch=1,
            grid=(1,),
            in_specs=[
                pl.BlockSpec((1, ext_rows, width), lambda s, p: (which, 0, 0)),
                pl.BlockSpec(bias.shape, lambda s, p: (0, 0, 0)),
            ]
            + [pl.BlockSpec(memory_space=pl.ANY)] * count,
            out_specs=pl.BlockSpec((1, rows, blocks * chan), lambda s, p: (s, 0, 0)),
            scratch_shapes=[
                pltpu.VMEM((count * slab, blocks * chan), BF),
                pltpu.SemaphoreType.DMA((count, blocks)),
            ],
        ),
        out_shape=jax.ShapeDtypeStruct((1, rows, blocks * chan), BF),
        compiler_params=params(),
        cost_estimate=pl.CostEstimate(
            flops=2 * rows * count * slab * blocks * chan,
            bytes_accessed=14_000_000,
            transcendentals=0,
        ),
        name="others",
    )(place, bases, bias, *part)


def pair_kernel(row, col, mask, pw, cot, row_out, sum_out, row_t, col_t, row_acc, *, batch):
    s, step = pl.program_id(0), pl.program_id(1)
    steps = pl.num_programs(1)
    many, wide, chan = cot.shape[1], cot.shape[2], cot.shape[3]
    pair_rows = row.shape[1]

    @pl.when(step == 0)
    def _():
        row_t[...] = row[0].T
        col_t[...] = col[0].T
        row_acc[...] = jnp.zeros_like(row_acc)
        sum_out[pl.ds(s, 1)] = jnp.zeros((1,) + sum_out.shape[1:], F32)

    @pl.when((step == 0) & (s == 0))
    def _():
        sum_out[batch] = jnp.zeros(sum_out.shape[1:], F32)

    lane = lax.broadcasted_iota(jnp.int32, (chan, pair_rows), 1)
    keep = mask[...].astype(F32)
    rows_now = row_t[...]
    acts, backs = [], []
    flat = cot[0].reshape(many * wide, chan)
    back = dot_nt(pw[...], flat)
    total = jnp.zeros((chan, wide), F32)
    row_sum = row_acc[...]
    for i in range(many):
        here = lane == step * many + i
        one = jnp.sum(jnp.where(here, rows_now, 0.0), axis=1, keepdims=True)
        pre = col_t[...] + one
        act, slope = gelu_parts(pre)
        line = keep[i : i + 1]
        acts.append((act * line).astype(BF))
        grad = back[:, i * wide : (i + 1) * wide] * (slope * line)
        total = total + grad
        row_sum = row_sum + jnp.where(here, jnp.sum(grad, axis=1, keepdims=True), 0.0)
    row_acc[...] = row_sum
    sum_out[pl.ds(s, 1)] += total[None]
    sum_out[batch] += dot_nn(jnp.concatenate(acts, axis=1), flat)

    @pl.when(step == steps - 1)
    def _():
        row_out[0] = row_acc[...].T
        sum_out[pl.ds(s, 1)] = sum_out[pl.ds(s, 1)].reshape(sum_out.shape[1:]).T[None]


def pair(row, col, mask, pw, cot):
    batch, rows, cols, chan = cot.shape
    many = 16
    return pl.pallas_call(
        functools.partial(pair_kernel, batch=batch),
        grid=(batch, rows // many),
        in_specs=[
            pl.BlockSpec((1, rows, chan), lambda s, i: (s, 0, 0)),
            pl.BlockSpec((1, cols, chan), lambda s, i: (s, 0, 0)),
            pl.BlockSpec((many, cols), lambda s, i: (i, 0)),
            pl.BlockSpec(pw.shape, lambda s, i: (0, 0)),
            pl.BlockSpec((1, many, cols, chan), lambda s, i: (s, i, 0, 0)),
        ],
        out_specs=[
            pl.BlockSpec((1, rows, chan), lambda s, i: (s, 0, 0)),
            pl.BlockSpec((batch + 1, cols, chan), lambda s, i: (0, 0, 0)),
        ],
        out_shape=[
            jax.ShapeDtypeStruct((batch, rows, chan), F32),
            jax.ShapeDtypeStruct((batch + 1, cols, chan), F32),
        ],
        scratch_shapes=[
            pltpu.VMEM((chan, rows), F32),
            pltpu.VMEM((chan, cols), F32),
            pltpu.VMEM((chan, rows), F32),
        ],
        compiler_params=params(),
        cost_estimate=pl.CostEstimate(
            flops=30 * batch * rows * cols * chan * 16, bytes_accessed=5_000_000, transcendentals=0
        ),
        name="pair",
    )(row, col, mask, pw, cot)


def hot_grad_kernel(bases, slope, both, proj, out, acc, *, taps, pool):
    chan = slope.shape[2]
    rows = slope.shape[1] - 2 * EDGE
    mid = taps // 2
    inner = EDGE // pool
    pg = dot_split(both[0], proj[...]) * (1.0 / pool)
    pg = spread(pg[inner : inner + rows // pool], pool)
    grad = (slope[0, EDGE : EDGE + rows, :].astype(F32) * pg).astype(BF)
    x = window_onehot(bases[0, EDGE : EDGE + rows + EDGE, :], WIN - EDGE - mid, rows, taps)
    part = dot_tn(grad, x)

    @pl.when(pl.program_id(0) == 0)
    def _():
        acc[...] = part

    @pl.when(pl.program_id(0) > 0)
    def _():
        acc[...] += part

    @pl.when(pl.program_id(0) == pl.num_programs(0) - 1)
    def _():
        out[...] = acc[...]


def hot_grad(bases, slope, both, proj, taps, pool):
    batch, ext_rows, width = bases.shape
    rows, chan = slope.shape[1:]
    wide = taps * width * 4
    return pl.pallas_call(
        functools.partial(hot_grad_kernel, taps=taps, pool=pool),
        grid=(batch,),
        in_specs=[
            pl.BlockSpec((1, ext_rows, width), lambda s: (s, 0, 0)),
            pl.BlockSpec((1, rows, chan), lambda s: (s, 0, 0)),
            pl.BlockSpec((1,) + both.shape[1:], lambda s: (s, 0, 0)),
            pl.BlockSpec(proj.shape, lambda s: (0, 0)),
        ],
        out_specs=pl.BlockSpec((chan, wide), lambda s: (0, 0)),
        out_shape=jax.ShapeDtypeStruct((chan, wide), F32),
        scratch_shapes=[pltpu.VMEM((chan, wide), F32)],
        compiler_params=params(),
        cost_estimate=pl.CostEstimate(
            flops=2 * batch * rows * wide * chan, bytes_accessed=6_000_000, transcendentals=0
        ),
        name="hot_grad",
    )(bases, slope, both, proj)


def unfold_kernel(place, *refs, taps, steps):
    parts = refs[:4]
    stem, out, hot = refs[4:]
    bits = stem.shape[0]
    rows, cut = parts[0].shape
    mine = pl.program_id(0) == 0
    piece = rows >> len(steps)
    for side in range(2):
        order = steps if side == 0 else steps[::-1]
        value = jnp.where(mine, parts[side][...], parts[2 + side][...])
        for r in range(rows // piece):
            first = 0
            for at, step in enumerate(order):
                own = lax.rem(place[2] // step, 2)
                away = (r >> (len(order) - 1 - at)) & 1
                first = first + (own ^ away) * (rows >> (at + 1))
            hot[pl.ds(pl.multiple_of(first, 16), piece), side * cut : (side + 1) * cut] = value[
                r * piece : (r + 1) * piece
            ]
    for t in range(taps):
        out[t] = dot_nn(hot[:, t * bits : (t + 1) * bits], stem[...]).astype(BF)


def unfold(place, parts, stem, taps):
    rows, cut = parts[0].shape
    bits, full = stem.shape
    steps = powers(lax.axis_size("seq"))[1:]
    return pl.pallas_call(
        functools.partial(unfold_kernel, taps=taps, steps=steps),
        grid_spec=pltpu.PrefetchScalarGridSpec(
            num_scalar_prefetch=1,
            grid=(2,),
            in_specs=[pl.BlockSpec((rows, cut), lambda h, p: (0, 0))] * 4
            + [pl.BlockSpec((bits, full), lambda h, p: (0, 0))],
            out_specs=pl.BlockSpec((taps, rows, full), lambda h, p: (0, p[1] ^ h, 0)),
            scratch_shapes=[pltpu.VMEM((rows, 2 * cut), BF)],
        ),
        out_shape=jax.ShapeDtypeStruct((taps, 2 * rows, full), BF),
        compiler_params=params(),
        cost_estimate=pl.CostEstimate(
            flops=4 * taps * rows * bits * full, bytes_accessed=9_000_000, transcendentals=0
        ),
        name="unfold",
    )(place, *parts, stem)


def token_kernel(
    place, slope, slopes, *refs, taps, pool, tiles, pieces
):
    w_other = refs[:pieces]
    both, proj, w_own = refs[pieces : pieces + 3]
    out, w_all, grads, y, sems = refs[-5:]
    cols, chan = proj.shape[0], proj.shape[2]
    ext = slope.shape[1]
    rows = ext - 2 * EDGE
    pick = both.shape[2]
    mid = taps // 2
    b = place[0]
    slab = chan // pieces

    copies = []
    for t in range(taps):
        lanes = slice(t * chan, (t + 1) * chan)
        own = w_own.at[t, :, pl.ds(pl.multiple_of(b * chan, 128), chan)]
        copies.append(pltpu.make_async_copy(own, w_all.at[0:chan, lanes], sems.at[pieces, 0, t]))
        for r in range(pieces):
            first = pl.multiple_of((place[2] ^ r) * slab, 16)
            for q in range(1, cols):
                copies.append(
                    pltpu.make_async_copy(
                        w_other[r].at[q - 1, t],
                        w_all.at[pl.ds(q * chan + first, slab), lanes],
                        sems.at[r, q - 1, t],
                    )
                )
    for copy in copies:
        copy.start()
    for copy in copies:
        copy.wait()

    total = None
    for q in range(cols):
        pg = spread(dot_split(both[0], proj[q, 0:pick, :]) * (1.0 / pool), pool)
        lanes = slice(q * chan, (q + 1) * chan)
        if q == 0:
            total = pg[EDGE : EDGE + rows]
            grads[:, lanes] = (slope[0].astype(F32) * pg).astype(BF)
            continue
        held = slopes[0, :, (q - 1) * chan : q * chan]
        grads[:, lanes] = (held.astype(F32) * pg).astype(BF)
    step = ext // tiles
    for first in range(0, taps, 2):
        some = min(2, taps - first)
        for i in range(tiles):
            y[i * step : (i + 1) * step, 0 : some * chan] = dot_nn(
                grads[i * step : (i + 1) * step, :],
                w_all[:, first * chan : (first + some) * chan],
            )
        for t in range(first, first + some):
            at = EDGE + mid - t
            total = total + y[at : at + rows, (t - first) * chan : (t - first + 1) * chan]
    out[0] = total.astype(BF)


def token(place, slope, slopes, both, proj, w_own, w_other, pool, which, earlier):
    batch, ext, chan = slope.shape
    taps = w_own.shape[0]
    cols = proj.shape[0]
    rows = ext - 2 * EDGE
    here = lambda s, p: (which, 0, 0)
    more = [] if earlier is None else [earlier]
    return pl.pallas_call(
        functools.partial(
            token_kernel, taps=taps, pool=pool, tiles=row_tiles(ext), pieces=len(w_other)
        ),
        grid_spec=pltpu.PrefetchScalarGridSpec(
            num_scalar_prefetch=1,
            grid=(1,),
            in_specs=[
                pl.BlockSpec((1, ext, chan), here),
                pl.BlockSpec(slopes[which].shape, lambda s, p: (0, 0, 0)),
                *[pl.BlockSpec(memory_space=pl.ANY) for _ in w_other],
                pl.BlockSpec((1,) + both.shape[1:], here),
                pl.BlockSpec(proj.shape, lambda s, p: (0, 0, 0)),
                pl.BlockSpec(memory_space=pl.ANY),
                *[pl.BlockSpec(memory_space=pl.ANY) for _ in more],
            ],
            out_specs=pl.BlockSpec((1, rows, chan), here),
            scratch_shapes=[
                pltpu.VMEM((cols * chan, taps * chan), BF),
                pltpu.VMEM((ext, cols * chan), BF),
                pltpu.VMEM((ext, 2 * chan), F32),
                pltpu.SemaphoreType.DMA((len(w_other) + 1, cols - 1, taps)),
            ],
        ),
        out_shape=jax.ShapeDtypeStruct((batch, rows, chan), BF),
        compiler_params=params(),
        cost_estimate=pl.CostEstimate(
            flops=2 * ext * cols * chan * taps * chan,
            bytes_accessed=16_000_000,
            transcendentals=0,
        ),
        input_output_aliases={6 + len(w_other): 0} if more else {},
        name="token",
    )(place, slope, slopes[which], *w_other, both, proj, w_own, *more)


def plain_fold(stem_full, weight):
    bits, full = stem_full.shape
    taps, chan, _ = weight.shape
    stem = stem_full.reshape(bits // 4, 4, full).transpose(1, 0, 2).reshape(bits, full)
    m = jnp.einsum("kc,toc->tko", stem, weight, preferred_element_type=F32).astype(BF)
    return stem, m.reshape(taps * bits, chan)


def plain_hot(bases, rows, taps):
    first = WIN - EDGE - taps // 2
    return jax.vmap(lambda one: window_onehot(one, first, rows, taps))(bases)


def plain_pair(row, col, mask, pw, cot):
    act, slope = gelu_parts(row[:, :, None, :] + col[:, None, :, :])
    masked = cot * mask[None, :, :, None].astype(BF)
    wg = jnp.einsum("bmnp,bmnq->pq", act.astype(BF), masked, preferred_element_type=F32)
    grad = jnp.einsum("bmnq,pq->bmnp", masked, pw, preferred_element_type=F32) * slope
    return grad.sum(2), grad.sum(1), wg


def per_device(
    bases, stem_weight, conv_weight, conv_bias, pair_proj, pair_weight, pair_cotangent, pair_mask
):
    batch, tok_rows, width = bases.shape
    taps, chan, full = conv_weight.shape
    pair_rows, pair_cols = pair_cotangent.shape[1:3]
    pair_chan = pair_weight.shape[0]
    pool = tok_rows // pair_rows
    bits = stem_weight.shape[0]
    ns, nc = lax.axis_size("seq"), lax.axis_size("col")
    a, b = lax.axis_index("seq"), lax.axis_index("col")
    core = lax.rem(a, 2)
    place = jnp.stack([b, core, a]).astype(jnp.int32)
    tiled = chan % 128 == 0 and pair_cols % 128 == 0
    ext_rows = tok_rows + 2 * EDGE
    near = [r for r in range(2, ns, 2) if r & (r - 1) == 0]
    far = [r for r in range(2, ns, 2) if r & (r - 1) != 0]
    odd = list(range(1, ns, 2))
    seq_steps, col_steps = powers(ns), powers(nc)
    join = lax.optimization_barrier

    def up(x):
        return lax.ppermute(x, "seq", [(i, i + 1) for i in range(ns - 1)])

    def down(x):
        return lax.ppermute(x, "seq", [(i + 1, i) for i in range(ns - 1)])

    def from_col(x, k):
        return lax.ppermute(x, "col", [(i, (i - k) % nc) for i in range(nc)])

    def slabs(part, chosen):
        for r in chosen:
            low_bit = r & -r
            part[r] = lax.ppermute(part[r - low_bit], "seq", xor_pairs(ns, low_bit))
        return [part[r] for r in chosen]

    def put(part, chosen, values):
        part.update(zip(chosen, values))

    half = lax.dynamic_slice_in_dim(stem_weight, core * (bits // 2), bits // 2, 0)
    mine = [from_col(half, k) for k in range(1, nc)]
    marked = bases + 1
    ends = [up(marked[:, tok_rows - WIN :]), down(marked[:, :WIN])]
    hi = conv_bias.astype(BF)
    rest = conv_bias - hi.astype(F32)
    mid = rest.astype(BF)
    low = (rest - mid.astype(F32)).astype(BF)
    tail = jnp.concatenate([jnp.stack([hi, mid, low]), jnp.zeros((13, chan), BF)])
    proj_own = jnp.concatenate([pair_proj.T, tail])
    slab = chan // ns
    rows_now = lax.dynamic_slice_in_dim(conv_weight, a * slab, slab, 1)
    blocks = [
        lax.dynamic_slice_in_dim(rows_now, lax.rem(b - k + nc, nc) * chan, chan, 2)
        for k in range(1, nc)
    ]
    mine, ends, proj_own, blocks = join((jnp.stack(mine), ends, proj_own, blocks))

    other = lax.ppermute(mine, "seq", xor_pairs(ns, 1))
    ext = jnp.concatenate([ends[0], marked, ends[1]], axis=1)
    turned = {0: [from_col(block, k) for k, block in enumerate(blocks, 1)]}
    other, ext = join((other, ext))

    if tiled:
        stem, stem_own, m = fold(place, stem_weight, mine, other, conv_weight)
    else:
        stem_full = lax.all_gather(stem_weight, "col", axis=1, tiled=True)
        stem, m = plain_fold(stem_full, conv_weight)
        stem_own = lax.dynamic_slice_in_dim(stem, b * chan, chan, 1)
    m_slab = taps * bits // ns
    stem, stem_own, m, turned[0] = join((stem, stem_own, m, turned[0]))
    turned[0] = jnp.stack(turned[0])

    mine_m = lax.dynamic_slice_in_dim(m, a * m_slab, m_slab, 0)
    part = {0: [from_col(mine_m, k) for k in range(1, nc)]}
    slabs(turned, near)
    if tiled:
        slope, proj_part = forward(ext, m, stem_own, conv_bias[None], pair_proj, taps, pool)
    else:
        hot = plain_hot(ext, ext_rows, taps)
        conv = jnp.einsum("brk,ko->bro", hot, m, preferred_element_type=F32) + conv_bias
        center = hot[:, :, taps // 2 * bits : (taps // 2 + 1) * bits]
        embedded = jnp.einsum("brk,kc->brc", center, stem_own, preferred_element_type=F32)
        act, slope = gelu_parts(conv)
        slope = slope.astype(BF)
        feats = (embedded.astype(BF).astype(F32) + act).astype(BF)[:, EDGE : EDGE + tok_rows]
        pooled = feats.astype(F32).reshape(batch, pair_rows, pool, chan).mean(2)
        proj_part = jnp.einsum(
            "bmc,cp->bmp", pooled, pair_proj.astype(F32), precision=lax.Precision.HIGHEST
        )
    slope, proj_part, part[0], got = join((slope, proj_part, part[0], [turned[r] for r in near]))
    put(turned, near, got)
    part[0] = jnp.stack(part[0])

    slabs(part, near)
    projected = sum_over(proj_part, "col")
    projected, got = join((projected, [part[r] for r in near]))
    put(part, near, got)
    row_feat = projected[..., :pair_chan]
    col_own = projected[..., pair_chan:]
    wide = jnp.pad(col_own, ((0, 0), (pair_cols, pair_cols), (0, 0)))
    at = jnp.clip(pair_cols - (a * pair_rows - b * pair_cols), 0, pair_cols + pair_rows)
    col_feat = sum_over(lax.dynamic_slice_in_dim(wide, at, pair_cols, 1), "seq")
    row_feat, col_feat = join((row_feat, col_feat))

    slabs(part, far)
    projs = [proj_own] + [from_col(proj_own, k) for k in range(1, nc)]
    if tiled:
        row_part, sums = pair(row_feat, col_feat, pair_mask, pair_weight, pair_cotangent)
    else:
        row_part, col_part, wg = plain_pair(
            row_feat, col_feat, pair_mask, pair_weight, pair_cotangent
        )
        sums = jnp.concatenate([col_part, wg.reshape(-1, pair_cols, pair_chan)], axis=0)
    row_part, sums, projs, got = join((row_part, sums, projs, [part[r] for r in far]))
    put(part, far, got)
    projs = jnp.stack(projs)

    slabs(part, odd)
    sums = swap_add(sums, "seq", seq_steps[0])
    row_grad = swap_add(row_part, "col", col_steps[0])
    sums, row_grad, got = join((sums, row_grad, [part[r] for r in odd]))
    put(part, odd, got)
    part = [part[r] for r in range(ns)]
    slopes = []
    slabs(turned, far)
    sums = swap_add(sums, "seq", seq_steps[1])
    row_grad = sum_over(row_grad, "col", 1)
    if tiled:
        slopes.append(others(place, ext, projs, part, taps, 0))
    sums, row_grad, slopes, got = join((sums, row_grad, slopes, [turned[r] for r in far]))
    put(turned, far, got)
    slabs(turned, odd)
    for step in seq_steps[2:]:
        sums = swap_add(sums, "seq", step)
    row_ext = jnp.concatenate([up(row_grad[:, pair_rows - 1 :]), row_grad, down(row_grad[:, :1])], axis=1)
    if tiled:
        slopes.append(others(place, ext, projs, part, taps, 1))
    sums, row_ext, slopes, got = join((sums, row_ext, slopes, [turned[r] for r in odd]))
    put(turned, odd, got)
    turned = [turned[r] for r in range(ns)]
    sums = sums.reshape(-1, pair_chan)
    col_block = sums[: batch * pair_cols].reshape(batch, pair_cols, pair_chan)
    need = pair_rows + 2
    wide = jnp.pad(col_block, ((0, 0), (need, need), (0, 0)))
    at = jnp.clip(a * pair_rows - 1 - b * pair_cols + need, 0, pair_cols + need)
    col_now = lax.dynamic_slice_in_dim(wide, at, need, 1).reshape(batch * need, pair_chan)
    last = sum_over(jnp.concatenate([sums[batch * pair_cols :], col_now]), "col")
    pair_weight_grad = last[:pair_chan]
    col_ext = last[pair_chan:].reshape(batch, need, pair_chan)
    both = jnp.concatenate([row_ext, col_ext], axis=-1)

    if tiled:
        hot_part = hot_grad(ext, slope, both, proj_own[: 2 * pair_chan], taps, pool)
    else:
        pg = jnp.einsum(
            "bmp,npc->nbmc",
            both,
            projs[:, : 2 * pair_chan].astype(F32),
            precision=lax.Precision.HIGHEST,
        )
        pg = jnp.repeat(pg, pool, axis=2)[:, :, pool - EDGE : pool - EDGE + ext_rows] / pool
        grad = (slope.astype(F32) * pg[0]).astype(BF)[:, EDGE : EDGE + tok_rows]
        hot_part = jnp.einsum(
            "bro,brk->ok", grad, hot[:, EDGE : EDGE + tok_rows], preferred_element_type=F32
        )
    hot_part = join((hot_part, both))[0]

    if tiled:
        beside = [
            functools.partial(token, place, slope, slopes, both, projs, conv_weight, turned, pool, s)
            for s in range(batch)
        ]
        hot_sum, token_grad = reduce_hot(hot_part, a, ns, beside)
        conv_weight_grad = unfold(place, hot_sum, stem, taps)
    else:
        hot_sum = lax.psum(hot_part, "seq").astype(BF)
        order = a ^ jnp.arange(ns)
        m_all = jnp.stack(part)[order].transpose(1, 0, 2, 3).reshape(nc - 1, taps * bits, chan)
        w_all = jnp.stack(turned)[order].transpose(1, 2, 0, 3, 4).reshape(nc - 1, taps, chan, chan)
        w_own = lax.dynamic_slice_in_dim(conv_weight, b * chan, chan, 2)
        total = pg[0, :, EDGE : EDGE + tok_rows]
        for q in range(nc):
            if q == 0:
                held, w_q = slope, w_own
            else:
                tail = projs[q, -16:].astype(F32)
                conv = jnp.einsum("brk,ko->bro", hot, m_all[q - 1], preferred_element_type=F32)
                held = gelu_parts(conv + (tail[0] + tail[1] + tail[2]))[1].astype(BF)
                w_q = w_all[q - 1]
            grad = (held.astype(F32) * pg[q]).astype(BF)
            for t in range(taps):
                first = EDGE + taps // 2 - t
                total = total + jnp.einsum(
                    "bro,oc->brc", grad[:, first : first + tok_rows], w_q[t], preferred_element_type=F32
                )
        token_grad = total.astype(BF)
        conv_weight_grad = jnp.einsum(
            "otk,kc->toc", hot_sum.reshape(chan, taps, bits), stem, preferred_element_type=F32
        ).astype(BF)
    return (token_grad, conv_weight_grad, pair_weight_grad)


def reduce_hot(x, a, ns, beside):
    steps = powers(ns)
    join = lax.optimization_barrier

    def halves(v, step):
        size = v.shape[0] // 2
        bit = lax.rem(a // step, 2)
        keep = lax.dynamic_slice_in_dim(v, bit * size, size, 0)
        give = lax.dynamic_slice_in_dim(v, (1 - bit) * size, size, 0)
        got = lax.ppermute(give.astype(BF), "seq", xor_pairs(ns, step))
        return keep + got.astype(F32)

    def swap(v, step):
        return lax.ppermute(v, "seq", xor_pairs(ns, step))

    x = halves(x, steps[0])
    cut = x.shape[1] // 2
    one, two = x[:, :cut], x[:, cut:]
    rest = steps[1:]
    done = None
    calls = dict(zip([0, len(rest)], beside))
    for at, (i, j) in enumerate(zip(rest, rest[::-1])):
        one, two = halves(one, i), halves(two, j)
        if at in calls:
            done = calls[at](done)
        one, two, done = join((one, two, done))
    one, two = one.astype(BF), two.astype(BF)
    for at, (i, j) in enumerate(zip(rest[::-1], rest), len(rest)):
        got = swap(one, i), swap(two, j)
        if at in calls:
            done = calls[at](done)
        got, done = join((got, done))
        one, two = jnp.concatenate([one, got[0]]), jnp.concatenate([two, got[1]])
    for call in beside[2:]:
        done = call(done)
    return [one, two, swap(one, steps[0]), swap(two, steps[0])], done


def solution(mesh):
    placed = (
        P(None, "seq", None),
        P(None, "col"),
        P(None, "col", None),
        P("col"),
        P("col", None),
        P(),
        P(None, "seq", "col", None),
        P("seq", "col"),
    )
    return jax.shard_map(
        per_device,
        mesh=mesh,
        in_specs=placed,
        out_specs=(P(None, "seq", "col"), P(None, "col", None), P()),
        check_vma=False,
    )
```

```python
import functools

import jax
import jax.numpy as jnp
from jax import lax
from jax.experimental import pallas as pl
from jax.experimental.pallas import tpu as pltpu
from jax.sharding import PartitionSpec as P

BF, F32 = jnp.bfloat16, jnp.float32
EDGE = 16
WIN = 24
ROOT = 0.7978845608028654
CUBE = 0.044715


def gelu_parts(x):
    sq = x * x
    th = jnp.tanh(x * (ROOT + (ROOT * CUBE) * sq))
    half = 0.5 + 0.5 * th
    act = x * half
    return act, half + act * (1.0 - th) * (ROOT + (3.0 * ROOT * CUBE) * sq)


def dot_nn(a, b):
    return lax.dot_general(a, b, (((1,), (0,)), ((), ())), preferred_element_type=F32)


def dot_nt(a, b):
    return lax.dot_general(a, b, (((1,), (1,)), ((), ())), preferred_element_type=F32)


def dot_tn(a, b):
    return lax.dot_general(a, b, (((0,), (0,)), ((), ())), preferred_element_type=F32)


def dot_split(a, b, dot):
    hi = a.astype(BF)
    rest = a - hi.astype(F32)
    mid = rest.astype(BF)
    low = (rest - mid.astype(F32)).astype(BF)
    return dot(hi, b) + dot(mid, b) + dot(low, b)


def xor_pairs(count, step):
    return [(i, i ^ step) for i in range(count)]


def sum_over(x, axis, first=0):
    for step in powers(lax.axis_size(axis))[first:]:
        x = swap_add(x, axis, step)
    return x


def after(x, *earlier):
    return lax.optimization_barrier((x,) + earlier)[0]


def swap_add(x, axis, step):
    return x + lax.ppermute(x, axis, xor_pairs(lax.axis_size(axis), step))


def powers(count):
    steps = [1]
    while 2 * steps[-1] < count:
        steps.append(2 * steps[-1])
    return steps


def ring_order(count):
    return list(range(0, count, 2)) + list(range(1, count, 2))[::-1]


def ring_spots(count):
    order = ring_order(count)
    return [order.index(i) for i in range(count)]


def window_onehot(win, first, rows, taps, levels=4):
    parts = []
    for tap in range(taps):
        own = win[first + tap : first + tap + rows]
        for level in range(levels):
            parts.append(jnp.where(own == level + 1, 1.0, 0.0).astype(BF))
    return jnp.concatenate(parts, axis=1)


def spread(pg, pool):
    groups, chan = pg.shape
    return jnp.broadcast_to(pg[:, None, :], (groups, pool, chan)).reshape(groups * pool, chan)


def params(mebibytes):
    return pltpu.CompilerParams(vmem_limit_bytes=mebibytes * 1024 * 1024)


def fold_kernel(place, own, mine, other, w, stem_out, own_out, m_out, *, cols, spots):
    bits, chan = own.shape
    half = bits // 2
    per = bits // 4

    @pl.when(pl.program_id(0) == 0)
    def _():
        c = place[1]

        def pick(width, base):
            dst = lax.broadcasted_iota(jnp.int32, (bits, width), 0)
            src = 4 * (dst & (per - 1)) + (dst >> (per.bit_length() - 1))
            at = lax.broadcasted_iota(jnp.int32, (bits, width), 1) + base
            return jnp.where(src == at, 1.0, 0.0).astype(BF)

        own_p = dot_nn(pick(bits, 0), own[...]).astype(BF)
        own_out[...] = own_p
        pick_mine, pick_other = pick(half, half * c), pick(half, half * (1 - c))
        for j in range(cols):
            k = lax.rem(place[3] - spots[j] + cols, cols)
            at = jnp.maximum(k - 1, 0)
            got = dot_nn(pick_mine, mine[at]) + dot_nn(pick_other, other[at])
            stem_out[:, j * chan : (j + 1) * chan] = jnp.where(k == 0, own_p, got.astype(BF))

    m_out[...] = dot_nt(stem_out[...], w[0]).astype(BF)


def fold(place, own, mine, other, weight):
    taps, chan, full = weight.shape
    bits = own.shape[0]
    cols = full // chan
    whole = lambda t, p: (0, 0)
    whole3 = lambda t, p: (0, 0, 0)
    return pl.pallas_call(
        functools.partial(fold_kernel, cols=cols, spots=ring_spots(cols)),
        grid_spec=pltpu.PrefetchScalarGridSpec(
            num_scalar_prefetch=1,
            grid=(taps,),
            in_specs=[
                pl.BlockSpec(own.shape, whole),
                pl.BlockSpec(mine.shape, whole3),
                pl.BlockSpec(other.shape, whole3),
                pl.BlockSpec((1, chan, full), lambda t, p: (t, 0, 0)),
            ],
            out_specs=[
                pl.BlockSpec((bits, full), whole),
                pl.BlockSpec((bits, chan), whole),
                pl.BlockSpec((bits, chan), lambda t, p: (t, 0)),
            ],
        ),
        out_shape=[
            jax.ShapeDtypeStruct((bits, full), BF),
            jax.ShapeDtypeStruct((bits, chan), BF),
            jax.ShapeDtypeStruct((taps * bits, chan), BF),
        ],
        compiler_params=params(10),
        cost_estimate=pl.CostEstimate(
            flops=2 * taps * bits * chan * full, bytes_accessed=8_000_000, transcendentals=0
        ),
        name="fold",
    )(place, own, mine, other, weight)


def forward_kernel(bases, m, stem, bias, proj, slope_out, proj_out, *, tiles, taps, pool):
    rows = slope_out.shape[0] // tiles
    bits = stem.shape[0]
    mid = taps // 2
    pooled = []
    for i in range(tiles):
        win = bases[0, i * rows : i * rows + rows + EDGE, :]
        x = window_onehot(win, WIN - EDGE - mid, rows, taps)
        conv = dot_nn(x, m[...]) + bias[...]
        embedded = dot_nn(x[:, mid * bits : (mid + 1) * bits], stem[...]).astype(BF)
        act, slope = gelu_parts(conv)
        slope_out[i * rows : (i + 1) * rows, :] = slope.astype(BF)
        feats = (embedded.astype(F32) + act).astype(BF).astype(F32)
        pooled.append(feats.reshape(rows // pool, pool, feats.shape[1]).sum(1))
    pooled = jnp.concatenate(pooled, axis=0)
    inner = EDGE // pool
    pooled = pooled[inner : inner + proj_out.shape[0]] * (1.0 / pool)
    proj_out[...] = dot_split(pooled, proj[...], dot_nn)


def row_tiles(rows):
    for tiles in range(1, rows + 1):
        if rows % (tiles * 16) == 0 and rows // tiles <= 352:
            return tiles
    return 1


def forward(bases, m, stem, bias, proj, taps, pool, which):
    _, ext_rows, width = bases.shape
    rows = ext_rows - 2 * (WIN - EDGE)
    chan = stem.shape[1]
    pairs = (rows - 2 * EDGE) // pool
    two = lambda s: (0, 0)
    return pl.pallas_call(
        functools.partial(forward_kernel, tiles=row_tiles(rows), taps=taps, pool=pool),
        grid=(1,),
        in_specs=[
            pl.BlockSpec((1, ext_rows, width), lambda s: (which, 0, 0)),
            pl.BlockSpec(m.shape, two),
            pl.BlockSpec(stem.shape, two),
            pl.BlockSpec(bias.shape, two),
            pl.BlockSpec(proj.shape, two),
        ],
        out_specs=[
            pl.BlockSpec((rows, chan), two),
            pl.BlockSpec((pairs, proj.shape[1]), two),
        ],
        out_shape=[
            jax.ShapeDtypeStruct((rows, chan), BF),
            jax.ShapeDtypeStruct((pairs, proj.shape[1]), F32),
        ],
        compiler_params=params(10),
        cost_estimate=pl.CostEstimate(
            flops=2 * rows * m.shape[0] * chan, bytes_accessed=6_000_000, transcendentals=0
        ),
        name="forward",
    )(bases, m, stem, bias, proj)


def others_kernel(place, bases, bias, *refs, tiles, taps, pieces):
    part, out, m_all, sems = refs
    _, blocks, slab, chan = part.shape
    rows = out.shape[0] // tiles
    mid = taps // 2

    copies = []
    for r in range(pieces):
        for q in range(blocks):
            copies.append(
                pltpu.make_async_copy(
                    part.at[r, q],
                    m_all.at[r * slab : (r + 1) * slab, q * chan : (q + 1) * chan],
                    sems.at[r, q],
                )
            )
    for copy in copies:
        copy.start()

    line = jnp.concatenate([bias[q : q + 1] for q in range(blocks)], axis=1)
    for i in range(tiles):
        win = bases[0, i * rows : i * rows + rows + EDGE, :]
        x = window_onehot(win, WIN - EDGE - mid, rows, taps)
        if i == 0:
            for copy in copies:
                copy.wait()
        conv = dot_nn(x, m_all[...]) + line
        out[i * rows : (i + 1) * rows, :] = gelu_parts(conv)[1].astype(BF)


def others(place, bases, bias, part, taps, which):
    batch, ext_rows, width = bases.shape
    rows = ext_rows - 2 * (WIN - EDGE)
    count, blocks, slab, chan = part.shape
    return pl.pallas_call(
        functools.partial(
            others_kernel, tiles=row_tiles(rows), taps=taps, pieces=count
        ),
        grid_spec=pltpu.PrefetchScalarGridSpec(
            num_scalar_prefetch=1,
            grid=(1,),
            in_specs=[
                pl.BlockSpec((1, ext_rows, width), lambda s, p: (which, 0, 0)),
                pl.BlockSpec(bias.shape, lambda s, p: (0, 0)),
            ]
            + [pl.BlockSpec(memory_space=pl.ANY)],
            out_specs=pl.BlockSpec((rows, blocks * chan), lambda s, p: (0, 0)),
            scratch_shapes=[
                pltpu.VMEM((count * slab, blocks * chan), BF),
                pltpu.SemaphoreType.DMA((count, blocks)),
            ],
        ),
        out_shape=jax.ShapeDtypeStruct((rows, blocks * chan), BF),
        compiler_params=params(16),
        cost_estimate=pl.CostEstimate(
            flops=2 * rows * count * slab * blocks * chan,
            bytes_accessed=14_000_000,
            transcendentals=0,
        ),
        name="others",
    )(place, bases, bias, part)


def pair_kernel(row, col, mask, pw, cot, row_out, sum_out, row_t, col_t, row_acc, *, batch):
    s, step = pl.program_id(0), pl.program_id(1)
    steps = pl.num_programs(1)
    many, wide, chan = cot.shape[1], cot.shape[2], cot.shape[3]
    pair_rows = row.shape[1]

    @pl.when(step == 0)
    def _():
        row_t[...] = row[0].T
        col_t[...] = col[0].T
        row_acc[...] = jnp.zeros_like(row_acc)
        sum_out[pl.ds(s, 1)] = jnp.zeros((1,) + sum_out.shape[1:], F32)

    @pl.when((step == 0) & (s == 0))
    def _():
        sum_out[batch] = jnp.zeros(sum_out.shape[1:], F32)

    lane = lax.broadcasted_iota(jnp.int32, (chan, pair_rows), 1)
    keep = mask[...].astype(F32)
    rows_now = row_t[...]
    acts, backs = [], []
    flat = cot[0].reshape(many * wide, chan)
    back = dot_nt(pw[...], flat)
    total = jnp.zeros((chan, wide), F32)
    row_sum = row_acc[...]
    for i in range(many):
        here = lane == step * many + i
        one = jnp.sum(jnp.where(here, rows_now, 0.0), axis=1, keepdims=True)
        pre = col_t[...] + one
        act, slope = gelu_parts(pre)
        line = keep[i : i + 1]
        acts.append((act * line).astype(BF))
        grad = back[:, i * wide : (i + 1) * wide] * (slope * line)
        total = total + grad
        row_sum = row_sum + jnp.where(here, jnp.sum(grad, axis=1, keepdims=True), 0.0)
    row_acc[...] = row_sum
    sum_out[pl.ds(s, 1)] += total[None]
    sum_out[batch] += dot_nn(jnp.concatenate(acts, axis=1), flat)

    @pl.when(step == steps - 1)
    def _():
        row_out[0] = row_acc[...].T
        sum_out[pl.ds(s, 1)] = sum_out[pl.ds(s, 1)].reshape(sum_out.shape[1:]).T[None]


def pair(row, col, mask, pw, cot):
    batch, rows, cols, chan = cot.shape
    many = 16
    return pl.pallas_call(
        functools.partial(pair_kernel, batch=batch),
        grid=(batch, rows // many),
        in_specs=[
            pl.BlockSpec((1, rows, chan), lambda s, i: (s, 0, 0)),
            pl.BlockSpec((1, cols, chan), lambda s, i: (s, 0, 0)),
            pl.BlockSpec((many, cols), lambda s, i: (i, 0)),
            pl.BlockSpec(pw.shape, lambda s, i: (0, 0)),
            pl.BlockSpec((1, many, cols, chan), lambda s, i: (s, i, 0, 0)),
        ],
        out_specs=[
            pl.BlockSpec((1, rows, chan), lambda s, i: (s, 0, 0)),
            pl.BlockSpec((batch + 1, cols, chan), lambda s, i: (0, 0, 0)),
        ],
        out_shape=[
            jax.ShapeDtypeStruct((batch, rows, chan), F32),
            jax.ShapeDtypeStruct((batch + 1, cols, chan), F32),
        ],
        scratch_shapes=[
            pltpu.VMEM((chan, rows), F32),
            pltpu.VMEM((chan, cols), F32),
            pltpu.VMEM((chan, rows), F32),
        ],
        compiler_params=params(8),
        cost_estimate=pl.CostEstimate(
            flops=30 * batch * rows * cols * chan * 16, bytes_accessed=5_000_000, transcendentals=0
        ),
        name="pair",
    )(row, col, mask, pw, cot)


def hot_grad_kernel(bases, both, proj, *refs, taps, pool):
    slopes, out = refs[:-1], refs[-1]
    rows = slopes[0].shape[0] - 2 * EDGE
    mid = taps // 2
    inner = EDGE // pool
    for s, slope in enumerate(slopes):
        pg = dot_split(both[s], proj[...], dot_nt) * (1.0 / pool)
        pg = spread(pg[inner : inner + rows // pool], pool)
        grad = (slope[EDGE : EDGE + rows, :].astype(F32) * pg).astype(BF)
        x = window_onehot(bases[s, EDGE : EDGE + rows + EDGE, :], WIN - EDGE - mid, rows, taps)
        part = dot_tn(grad, x)
        if s == 0:
            out[...] = part
        else:
            out[...] += part


def hot_grad(bases, both, proj, slopes, taps, pool):
    width = bases.shape[2]
    rows, chan = slopes[0].shape
    wide = taps * width * 4
    return pl.pallas_call(
        functools.partial(hot_grad_kernel, taps=taps, pool=pool),
        out_shape=jax.ShapeDtypeStruct((chan, wide), F32),
        compiler_params=params(20),
        cost_estimate=pl.CostEstimate(
            flops=2 * len(slopes) * rows * wide * chan, bytes_accessed=6_000_000, transcendentals=0
        ),
        name="hot_grad",
    )(bases, both, proj, *slopes)


def unfold_kernel(place, *refs, taps, steps):
    parts = refs[:4]
    stem, out, hot = refs[4:]
    bits = stem.shape[0]
    rows, cut = parts[0].shape
    mine = pl.program_id(0) == 0
    piece = rows >> len(steps)
    for side in range(2):
        order = steps if side == 0 else steps[::-1]
        value = jnp.where(mine, parts[side][...], parts[2 + side][...])
        for r in range(rows // piece):
            first = 0
            for at, step in enumerate(order):
                own = lax.rem(place[2] // step, 2)
                away = (r >> (len(order) - 1 - at)) & 1
                first = first + (own ^ away) * (rows >> (at + 1))
            hot[pl.ds(pl.multiple_of(first, 16), piece), side * cut : (side + 1) * cut] = value[
                r * piece : (r + 1) * piece
            ]
    for t in range(taps):
        out[t] = dot_nn(hot[:, t * bits : (t + 1) * bits], stem[...]).astype(BF)


def unfold(place, parts, stem, taps):
    rows, cut = parts[0].shape
    bits, full = stem.shape
    steps = powers(lax.axis_size("seq"))[1:]
    return pl.pallas_call(
        functools.partial(unfold_kernel, taps=taps, steps=steps),
        grid_spec=pltpu.PrefetchScalarGridSpec(
            num_scalar_prefetch=1,
            grid=(2,),
            in_specs=[pl.BlockSpec((rows, cut), lambda h, p: (0, 0))] * 4
            + [pl.BlockSpec((bits, full), lambda h, p: (0, 0))],
            out_specs=pl.BlockSpec((taps, rows, full), lambda h, p: (0, p[1] ^ h, 0)),
            scratch_shapes=[pltpu.VMEM((rows, 2 * cut), BF)],
        ),
        out_shape=jax.ShapeDtypeStruct((taps, 2 * rows, full), BF),
        compiler_params=params(10),
        cost_estimate=pl.CostEstimate(
            flops=4 * taps * rows * bits * full, bytes_accessed=9_000_000, transcendentals=0
        ),
        name="unfold",
    )(place, *parts, stem)


def token_kernel(place, both, slope, slopes, *refs, cols, pieces, taps, pool, tiles):
    w_other, w_own, proj_own = refs[:3]
    out, w_all, grads, y, sems = refs[-5:]
    ext, chan = slope.shape
    rows = ext - 2 * EDGE
    mid = taps // 2
    slab = chan // pieces
    width = taps * chan
    firsts, copies = [], []
    for t in range(taps):
        copies.append(
            pltpu.make_async_copy(
                w_own.at[t, :, pl.ds(pl.multiple_of(place[0] * chan, 128), chan)],
                w_all.at[0:chan, t * chan : (t + 1) * chan],
                sems.at[pieces, t],
            )
        )
    for r in range(pieces):
        for q in range(1, cols):
            to = q * chan + r * slab
            for group, lanes, at in ((firsts, slice(width, None), 0), (copies, slice(0, width), 1)):
                group.append(
                    pltpu.make_async_copy(
                        w_other.at[r, q - 1, :, lanes],
                        w_all.at[to : to + slab, lanes],
                        sems.at[r, 2 * q + at],
                    )
                )
    for copy in firsts + copies:
        copy.start()
    for copy in firsts:
        copy.wait()

    own = None
    for q in range(cols):
        lanes = slice(q * chan, (q + 1) * chan)
        proj = proj_own[...] if q == 0 else w_all[lanes, width:]
        pg = spread(dot_split(both[0], proj, dot_nt) * (1.0 / pool), pool)
        if q == 0:
            own = pg[EDGE : EDGE + rows]
            now = slope[...]
        else:
            now = slopes[:, (q - 1) * chan : q * chan]
        grads[:, lanes] = (now.astype(F32) * pg).astype(BF)
    for copy in copies:
        copy.wait()
    step = ext // tiles
    for i in range(tiles):
        y[i * step : (i + 1) * step, :] = dot_nn(
            grads[i * step : (i + 1) * step, :], w_all[:, 0:width]
        )
    step = 128
    for i in range(0, rows, step):
        total = own[i : i + step]
        for t in range(taps):
            at = EDGE + mid - t + i
            total = total + y[at : at + step, t * chan : (t + 1) * chan]
        out[0, i : i + step, :] = total.astype(BF)


def token(place, both, slope, slopes, w_other, w_own, proj_own, pool, which, done):
    ext, chan = slope.shape
    taps = w_own.shape[0]
    cols = slopes.shape[1] // chan + 1
    rows = ext - 2 * EDGE
    whole = lambda s, p: (0, 0)
    here = lambda s, p: (which, 0, 0)
    batch = both.shape[0]
    anywhere = pl.BlockSpec(memory_space=pl.ANY)
    into = [] if done is None else [done]
    return pl.pallas_call(
        functools.partial(
            token_kernel, cols=cols, pieces=w_other.shape[0], taps=taps, pool=pool, tiles=row_tiles(ext)
        ),
        grid_spec=pltpu.PrefetchScalarGridSpec(
            num_scalar_prefetch=1,
            grid=(1,),
            in_specs=[
                pl.BlockSpec((1,) + both.shape[1:], here),
                pl.BlockSpec(slope.shape, whole),
                pl.BlockSpec(slopes.shape, whole),
                anywhere,
                anywhere,
                pl.BlockSpec(proj_own.shape, whole),
                *[anywhere for _ in into],
            ],
            out_specs=pl.BlockSpec((1, rows, chan), here),
            scratch_shapes=[
                pltpu.VMEM((cols * chan, w_other.shape[-1]), BF),
                pltpu.VMEM((ext, cols * chan), BF),
                pltpu.VMEM((ext, taps * chan), F32),
                pltpu.SemaphoreType.DMA((w_other.shape[0] + 1, max(taps, 2 * cols))),
            ],
        ),
        out_shape=jax.ShapeDtypeStruct((batch, rows, chan), BF),
        compiler_params=params(24),
        cost_estimate=pl.CostEstimate(
            flops=2 * ext * cols * chan * taps * chan, bytes_accessed=8_000_000, transcendentals=0
        ),
        input_output_aliases={7: 0} if into else {},
        name="token",
    )(place, both, slope, slopes, w_other, w_own, proj_own, *into)


def extended(block, sides, width):
    for axis, dim in sides:
        count = lax.axis_size(axis)
        forward = [(i, i + 1) for i in range(count - 1)]
        backward = [(target, source) for source, target in forward]
        low = lax.ppermute(
            lax.slice_in_dim(block, block.shape[dim] - width, None, axis=dim), axis, forward
        )
        high = lax.ppermute(lax.slice_in_dim(block, 0, width, axis=dim), axis, backward)
        block = jnp.concatenate([low, block, high], axis=dim)
    return block


def gelu_slope(values):
    return jax.vjp(jax.nn.gelu, values)[1](jnp.ones_like(values))[0]


def plain_device(
    bases, stem_weight, conv_weight, conv_bias, pair_proj, pair_weight, pair_cotangent, pair_mask
):
    batch, tok_rows, width_bp = bases.shape
    kernel = conv_weight.shape[0]
    chan_local = conv_weight.shape[1]
    pair_rows = pair_cotangent.shape[1]
    pair_cols = pair_cotangent.shape[2]
    pair_chan = pair_weight.shape[0]
    pool_len = tok_rows // pair_rows
    levels = jnp.arange(4, dtype=jnp.int32)
    onehot = (
        (bases[..., None] == levels).astype(jnp.bfloat16).reshape(batch, tok_rows, width_bp * 4)
    )
    embedded = jnp.einsum(
        "bik,kc->bic", onehot, stem_weight, preferred_element_type=jnp.float32
    ).astype(jnp.bfloat16)
    padded = extended(embedded, (("seq", 1),), 2)
    full_in = lax.all_gather(padded, "col", axis=2, tiled=True)
    conv_out = conv_bias[None, None, :]
    for tap in range(kernel):
        conv_out = conv_out + jnp.einsum(
            "bic,oc->bio",
            full_in[:, tap : tap + tok_rows],
            conv_weight[tap],
            preferred_element_type=jnp.float32,
        )
    features = (embedded.astype(jnp.float32) + jax.nn.gelu(conv_out)).astype(jnp.bfloat16)
    pooled = features.astype(jnp.float32).reshape(batch, pair_rows, pool_len, chan_local).mean(2)
    proj_f = pair_proj.astype(jnp.float32)
    proj_part = jnp.einsum("bmc,cp->bmp", pooled, proj_f, precision=lax.Precision.HIGHEST)
    projected = lax.psum(proj_part, "col")
    row_feat = projected[..., :pair_chan]
    col_own = projected[..., pair_chan:]
    col_every = lax.all_gather(col_own, "seq", axis=1, tiled=True)
    col_feat = lax.dynamic_slice_in_dim(col_every, lax.axis_index("col") * pair_cols, pair_cols, 1)
    pre_act = row_feat[:, :, None, :] + col_feat[:, None, :, :]
    activ = jax.nn.gelu(pre_act).astype(jnp.bfloat16)
    masked = pair_cotangent * pair_mask[None, :, :, None].astype(jnp.bfloat16)
    wgrad_part = jnp.einsum("bmnp,bmnq->pq", activ, masked, preferred_element_type=jnp.float32)
    pair_weight_grad = lax.psum(wgrad_part, ("seq", "col"))
    back = jnp.einsum("bmnq,pq->bmnp", masked, pair_weight, preferred_element_type=jnp.float32)
    pre_grad = back * gelu_slope(pre_act)
    row_grad = lax.psum(pre_grad.sum(2), "col")
    col_block = lax.psum(pre_grad.sum(1), "seq")
    col_whole = lax.all_gather(col_block, "col", axis=1, tiled=True)
    col_grad = lax.dynamic_slice_in_dim(col_whole, lax.axis_index("seq") * pair_rows, pair_rows, 1)
    both_grad = jnp.concatenate([row_grad, col_grad], axis=-1)
    pooled_grad = jnp.einsum("bmp,cp->bmc", both_grad, proj_f, precision=lax.Precision.HIGHEST)
    feat_grad = jnp.repeat(pooled_grad, pool_len, axis=1) / pool_len
    conv_grad = (feat_grad * gelu_slope(conv_out)).astype(jnp.bfloat16)
    weight_part = jnp.stack(
        [
            jnp.einsum(
                "bio,bic->oc",
                conv_grad,
                full_in[:, tap : tap + tok_rows],
                preferred_element_type=jnp.float32,
            )
            for tap in range(kernel)
        ]
    )
    conv_weight_grad = lax.psum(weight_part, "seq").astype(jnp.bfloat16)
    grad_pad = extended(conv_grad, (("seq", 1),), 2)
    turned = lax.all_to_all(conv_weight, "col", split_axis=2, concat_axis=1, tiled=True)
    empty = jnp.zeros((batch, tok_rows, chan_local), jnp.float32)
    total = empty
    piece = lax.all_gather(grad_pad, "col", axis=2, tiled=True)
    for tap in range(kernel):
        total = total + jnp.einsum(
            "bjo,oc->bjc",
            piece[:, 4 - tap : 4 - tap + tok_rows],
            turned[tap],
            preferred_element_type=jnp.float32,
        )
    token_grad = (feat_grad + total).astype(jnp.bfloat16)
    return (token_grad, conv_weight_grad, pair_weight_grad)


def per_device(
    bases, stem_weight, conv_weight, conv_bias, pair_proj, pair_weight, pair_cotangent, pair_mask
):
    batch, tok_rows, width = bases.shape
    taps, chan, full = conv_weight.shape
    pair_rows, pair_cols = pair_cotangent.shape[1:3]
    pair_chan = pair_weight.shape[0]
    pool = tok_rows // pair_rows
    bits = stem_weight.shape[0]
    ns, nc = lax.axis_size("seq"), lax.axis_size("col")
    if chan % 128 or pair_cols % 128 or (chan // ns) % 16 or nc != 4 or batch != 2:
        return plain_device(
            bases, stem_weight, conv_weight, conv_bias, pair_proj, pair_weight, pair_cotangent,
            pair_mask,
        )
    a, b = lax.axis_index("seq"), lax.axis_index("col")
    core = lax.rem(a, 2)
    order, spots = ring_order(nc), ring_spots(nc)
    pick = lambda table: sum(jnp.where(b == i, v, 0) for i, v in enumerate(table))
    place = jnp.stack([b, core, a, pick(spots)]).astype(jnp.int32)
    near = [r for r in range(2, ns, 2) if r & (r - 1) == 0]
    far = [r for r in range(2, ns, 2) if r & (r - 1) != 0]
    odd = list(range(1, ns, 2))
    seq_steps = powers(ns)
    join = lax.optimization_barrier

    def up(x):
        return lax.ppermute(x, "seq", [(i, i + 1) for i in range(ns - 1)])

    def down(x):
        return lax.ppermute(x, "seq", [(i + 1, i) for i in range(ns - 1)])

    def ring(x, k):
        return lax.ppermute(x, "col", [(order[i], order[(i + k) % nc]) for i in range(nc)])

    def slabs(part, chosen):
        for r in chosen:
            low_bit = r & -r
            part[r] = lax.ppermute(part[r - low_bit], "seq", xor_pairs(ns, low_bit))
        return [part[r] for r in chosen]

    def put(part, chosen, values):
        part.update(zip(chosen, values))

    half = lax.dynamic_slice_in_dim(stem_weight, core * (bits // 2), bits // 2, 0)
    mine = [ring(half, k) for k in range(1, nc)]
    marked = bases + 1
    ends = [up(marked[:, tok_rows - WIN :]), down(marked[:, :WIN])]
    slab = chan // ns
    rows_now = lax.dynamic_slice_in_dim(conv_weight, a * slab, slab, 1)
    proj_now = lax.dynamic_slice_in_dim(pair_proj, a * slab, slab, 0)
    blocks = []
    for k in range(1, nc):
        to = pick([order[(spots[i] + k) % nc] for i in range(nc)])
        block = lax.dynamic_slice_in_dim(rows_now, to * chan, chan, 2)
        blocks.append(jnp.concatenate([block[t] for t in range(taps)] + [proj_now], axis=1))
    ext = jnp.concatenate([ends[0], marked, ends[1]], axis=1)
    mine, ext, blocks = join((mine, ext, blocks))
    mine = jnp.stack(mine)

    hi = conv_bias.astype(BF)
    rest = conv_bias - hi.astype(F32)
    mid = rest.astype(BF)
    low = (rest - mid.astype(F32)).astype(BF)
    tail = jnp.concatenate([jnp.stack([hi, mid, low]), jnp.zeros((13, chan), BF)])

    other = lax.ppermute(mine, "seq", xor_pairs(ns, 1))
    turned = [ring(block, k) for k, block in enumerate(blocks, 1)]
    stem, stem_own, m = join(fold(place, stem_weight, mine, other, conv_weight))

    bias = conv_bias[None]
    slope0, proj0 = forward(ext, m, stem_own, bias, pair_proj, taps, pool, 0)
    slope1, proj1 = forward(ext, m, stem_own, bias, pair_proj, taps, pool, 1)
    slope0, slope1, proj0, proj1, turned, m = join((slope0, slope1, proj0, proj1, turned, m))
    turned = lax.all_gather(jnp.stack(turned), "seq", axis=0)

    projected = swap_add(jnp.stack([proj0, proj1]), "col", 1)
    projected, m = join((sum_over(projected, "col", 1), m))
    m_slab = taps * bits // ns
    mine_m = jnp.concatenate([lax.dynamic_slice_in_dim(m, a * m_slab, m_slab, 0), tail])
    part = [ring(mine_m, k) for k in range(1, nc)]
    row_feat = projected[..., :pair_chan]
    col_own = projected[..., pair_chan:]
    wide = jnp.pad(col_own, ((0, 0), (pair_cols, pair_cols), (0, 0)))
    at = jnp.clip(pair_cols - (a * pair_rows - b * pair_cols), 0, pair_cols + pair_rows)
    col_feat = sum_over(lax.dynamic_slice_in_dim(wide, at, pair_cols, 1), "seq")
    row_feat, col_feat = join((row_feat, col_feat))

    row_part, sums = pair(row_feat, col_feat, pair_mask, pair_weight, pair_cotangent)
    row_part, sums, part = join((row_part, sums, part))
    biases = jnp.stack([one[m_slab : m_slab + 3].astype(F32).sum(0) for one in part])
    part = lax.all_gather(jnp.stack([one[:m_slab] for one in part]), "seq", axis=0)

    sums = swap_add(sums, "seq", seq_steps[0])
    row_grad = swap_add(row_part, "col", 1)
    sums, row_grad = join((sums, row_grad))
    sums = swap_add(sums, "seq", seq_steps[1])
    row_grad = sum_over(row_grad, "col", 1)
    sums, row_grad = join((sums, row_grad))
    for step in seq_steps[2:]:
        sums = swap_add(sums, "seq", step)
    row_ext = jnp.concatenate(
        [up(row_grad[:, pair_rows - 1 :]), row_grad, down(row_grad[:, :1])], axis=1
    )
    sums, row_ext = join((sums, row_ext))
    sums = sums.reshape(-1, pair_chan)
    col_block = sums[: batch * pair_cols].reshape(batch, pair_cols, pair_chan)
    need = pair_rows + 2
    wide = jnp.pad(col_block, ((0, 0), (need, need), (0, 0)))
    at = jnp.clip(a * pair_rows - 1 - b * pair_cols + need, 0, pair_cols + need)
    col_now = lax.dynamic_slice_in_dim(wide, at, need, 1).reshape(batch * need, pair_chan)
    last = sum_over(jnp.concatenate([sums[batch * pair_cols :], col_now]), "col")
    pair_weight_grad = last[:pair_chan]
    col_ext = last[pair_chan:].reshape(batch, need, pair_chan)
    both = jnp.concatenate([row_ext, col_ext], axis=-1)
    both = join(both)

    hot_part = hot_grad(ext, both, pair_proj, [slope0, slope1], taps, pool)
    hot_part, both, turned, part = join((hot_part, both, turned, part))

    def slopes_of(s):
        return lambda done: (done and done[0], others(place, ext, biases, part, taps, s))

    def tokens(s):
        slope = (slope0, slope1)[s]
        return lambda done: (
            token(place, both, slope, done[1], turned, conv_weight, pair_proj, pool, s, done[0]),
            None,
        )

    beside = [slopes_of(0), tokens(0), slopes_of(1), tokens(1)]
    hot_sum, token_grad = reduce_hot(hot_part, a, ns, beside)
    conv_weight_grad = unfold(place, hot_sum, stem, taps)
    return (token_grad, conv_weight_grad, pair_weight_grad)


def reduce_hot(x, a, ns, beside):
    steps = powers(ns)
    join = lax.optimization_barrier

    def halves(v, step):
        size = v.shape[0] // 2
        bit = lax.rem(a // step, 2)
        keep = lax.dynamic_slice_in_dim(v, bit * size, size, 0)
        give = lax.dynamic_slice_in_dim(v, (1 - bit) * size, size, 0)
        got = lax.ppermute(give.astype(BF), "seq", xor_pairs(ns, step))
        return keep + got.astype(F32)

    def swap(v, step):
        return lax.ppermute(v, "seq", xor_pairs(ns, step))

    x = halves(x, steps[0])
    cut = x.shape[1] // 2
    one, two = x[:, :cut], x[:, cut:]
    rest = steps[1:]
    done = None
    calls = dict(enumerate(beside))
    for at, (i, j) in enumerate(zip(rest, rest[::-1])):
        one, two = halves(one, i), halves(two, j)
        if at in calls:
            done = calls[at](done)
        one, two, done = join((one, two, done))
    one, two = one.astype(BF), two.astype(BF)
    for at, (i, j) in enumerate(zip(rest[::-1], rest), len(rest)):
        got = swap(one, i), swap(two, j)
        if at in calls:
            done = calls[at](done)
        got, done = join((got, done))
        one, two = jnp.concatenate([one, got[0]]), jnp.concatenate([two, got[1]])
    return [one, two, swap(one, steps[0]), swap(two, steps[0])], done[0]


def solution(mesh):
    placed = (
        P(None, "seq", None),
        P(None, "col"),
        P(None, "col", None),
        P("col"),
        P("col", None),
        P(),
        P(None, "seq", "col", None),
        P("seq", "col"),
    )
    return jax.shard_map(
        per_device,
        mesh=mesh,
        in_specs=placed,
        out_specs=(P(None, "seq", "col"), P(None, "col", None), P()),
        check_vma=False,
    )
```

```python
import functools

import jax
import jax.numpy as jnp
from jax import lax
from jax.experimental import pallas as pl
from jax.experimental.pallas import tpu as pltpu
from jax.sharding import PartitionSpec as P

BF, F32 = jnp.bfloat16, jnp.float32
EDGE = 16
WIN = 24
ROOT = 0.7978845608028654
CUBE = 0.044715


def gelu_parts(x):
    sq = x * x
    th = jnp.tanh(x * (ROOT + (ROOT * CUBE) * sq))
    half = 0.5 + 0.5 * th
    act = x * half
    return act, half + act * (1.0 - th) * (ROOT + (3.0 * ROOT * CUBE) * sq)


def dot_nn(a, b):
    return lax.dot_general(a, b, (((1,), (0,)), ((), ())), preferred_element_type=F32)


def dot_nt(a, b):
    return lax.dot_general(a, b, (((1,), (1,)), ((), ())), preferred_element_type=F32)


def dot_tn(a, b):
    return lax.dot_general(a, b, (((0,), (0,)), ((), ())), preferred_element_type=F32)


def dot_split(a, b, dot):
    hi = a.astype(BF)
    rest = a - hi.astype(F32)
    mid = rest.astype(BF)
    low = (rest - mid.astype(F32)).astype(BF)
    return dot(hi, b) + dot(mid, b) + dot(low, b)


def xor_pairs(count, step):
    return [(i, i ^ step) for i in range(count)]


def sum_over(x, axis, first=0):
    for step in powers(lax.axis_size(axis))[first:]:
        x = swap_add(x, axis, step)
    return x


def after(x, *earlier):
    return lax.optimization_barrier((x,) + earlier)[0]


def swap_add(x, axis, step):
    return x + lax.ppermute(x, axis, xor_pairs(lax.axis_size(axis), step))


def powers(count):
    steps = [1]
    while 2 * steps[-1] < count:
        steps.append(2 * steps[-1])
    return steps


def ring_order(count):
    return list(range(0, count, 2)) + list(range(1, count, 2))[::-1]


def ring_spots(count):
    order = ring_order(count)
    return [order.index(i) for i in range(count)]


def window_onehot(win, first, rows, taps, levels=4):
    parts = []
    for tap in range(taps):
        own = win[first + tap : first + tap + rows]
        for level in range(levels):
            parts.append(jnp.where(own == level + 1, 1.0, 0.0).astype(BF))
    return jnp.concatenate(parts, axis=1)


def spread(pg, pool):
    groups, chan = pg.shape
    return jnp.broadcast_to(pg[:, None, :], (groups, pool, chan)).reshape(groups * pool, chan)


def params(mebibytes):
    return pltpu.CompilerParams(vmem_limit_bytes=mebibytes * 1024 * 1024)


def fold_kernel(place, own, mine, other, w, stem_out, own_out, m_out, *, cols, spots):
    bits, chan = own.shape
    half = bits // 2
    per = bits // 4

    @pl.when(pl.program_id(0) == 0)
    def _():
        c = place[1]

        def pick(width, base):
            dst = lax.broadcasted_iota(jnp.int32, (bits, width), 0)
            src = 4 * (dst & (per - 1)) + (dst >> (per.bit_length() - 1))
            at = lax.broadcasted_iota(jnp.int32, (bits, width), 1) + base
            return jnp.where(src == at, 1.0, 0.0).astype(BF)

        own_p = dot_nn(pick(bits, 0), own[...]).astype(BF)
        own_out[...] = own_p
        pick_mine, pick_other = pick(half, half * c), pick(half, half * (1 - c))
        for j in range(cols):
            k = lax.rem(place[3] - spots[j] + cols, cols)
            at = jnp.maximum(k - 1, 0)
            got = dot_nn(pick_mine, mine[at]) + dot_nn(pick_other, other[at])
            stem_out[:, j * chan : (j + 1) * chan] = jnp.where(k == 0, own_p, got.astype(BF))

    m_out[...] = dot_nt(stem_out[...], w[0]).astype(BF)


def fold(place, own, mine, other, weight):
    taps, chan, full = weight.shape
    bits = own.shape[0]
    cols = full // chan
    whole = lambda t, p: (0, 0)
    whole3 = lambda t, p: (0, 0, 0)
    return pl.pallas_call(
        functools.partial(fold_kernel, cols=cols, spots=ring_spots(cols)),
        grid_spec=pltpu.PrefetchScalarGridSpec(
            num_scalar_prefetch=1,
            grid=(taps,),
            in_specs=[
                pl.BlockSpec(own.shape, whole),
                pl.BlockSpec(mine.shape, whole3),
                pl.BlockSpec(other.shape, whole3),
                pl.BlockSpec((1, chan, full), lambda t, p: (t, 0, 0)),
            ],
            out_specs=[
                pl.BlockSpec((bits, full), whole),
                pl.BlockSpec((bits, chan), whole),
                pl.BlockSpec((bits, chan), lambda t, p: (t, 0)),
            ],
        ),
        out_shape=[
            jax.ShapeDtypeStruct((bits, full), BF),
            jax.ShapeDtypeStruct((bits, chan), BF),
            jax.ShapeDtypeStruct((taps * bits, chan), BF),
        ],
        compiler_params=params(10),
        cost_estimate=pl.CostEstimate(
            flops=2 * taps * bits * chan * full, bytes_accessed=8_000_000, transcendentals=0
        ),
        name="fold",
    )(place, own, mine, other, weight)


def forward_kernel(bases, m, stem, bias, proj, slope_out, proj_out, *, tiles, taps, pool):
    rows = slope_out.shape[0] // tiles
    bits = stem.shape[0]
    mid = taps // 2
    pooled = []
    for i in range(tiles):
        win = bases[0, i * rows : i * rows + rows + EDGE, :]
        x = window_onehot(win, WIN - EDGE - mid, rows, taps)
        conv = dot_nn(x, m[...]) + bias[...]
        embedded = dot_nn(x[:, mid * bits : (mid + 1) * bits], stem[...]).astype(BF)
        act, slope = gelu_parts(conv)
        slope_out[i * rows : (i + 1) * rows, :] = slope.astype(BF)
        feats = (embedded.astype(F32) + act).astype(BF).astype(F32)
        pooled.append(feats.reshape(rows // pool, pool, feats.shape[1]).sum(1))
    pooled = jnp.concatenate(pooled, axis=0)
    inner = EDGE // pool
    pooled = pooled[inner : inner + proj_out.shape[0]] * (1.0 / pool)
    proj_out[...] = dot_split(pooled, proj[...], dot_nn)


def row_tiles(rows):
    for tiles in range(1, rows + 1):
        if rows % (tiles * 16) == 0 and rows // tiles <= 352:
            return tiles
    return 1


def forward(bases, m, stem, bias, proj, taps, pool, which):
    _, ext_rows, width = bases.shape
    rows = ext_rows - 2 * (WIN - EDGE)
    chan = stem.shape[1]
    pairs = (rows - 2 * EDGE) // pool
    two = lambda s: (0, 0)
    return pl.pallas_call(
        functools.partial(forward_kernel, tiles=row_tiles(rows), taps=taps, pool=pool),
        grid=(1,),
        in_specs=[
            pl.BlockSpec((1, ext_rows, width), lambda s: (which, 0, 0)),
            pl.BlockSpec(m.shape, two),
            pl.BlockSpec(stem.shape, two),
            pl.BlockSpec(bias.shape, two),
            pl.BlockSpec(proj.shape, two),
        ],
        out_specs=[
            pl.BlockSpec((rows, chan), two),
            pl.BlockSpec((pairs, proj.shape[1]), two),
        ],
        out_shape=[
            jax.ShapeDtypeStruct((rows, chan), BF),
            jax.ShapeDtypeStruct((pairs, proj.shape[1]), F32),
        ],
        compiler_params=params(10),
        cost_estimate=pl.CostEstimate(
            flops=2 * rows * m.shape[0] * chan, bytes_accessed=6_000_000, transcendentals=0
        ),
        name="forward",
    )(bases, m, stem, bias, proj)


def others_kernel(place, bases, bias, *refs, tiles, taps, pieces):
    part, out, m_all, sems = refs
    _, blocks, slab, chan = part.shape
    rows = out.shape[0] // tiles
    mid = taps // 2

    copies = []
    for r in range(pieces):
        for q in range(blocks):
            copies.append(
                pltpu.make_async_copy(
                    part.at[r, q],
                    m_all.at[r * slab : (r + 1) * slab, q * chan : (q + 1) * chan],
                    sems.at[r, q],
                )
            )
    for copy in copies:
        copy.start()

    line = jnp.concatenate([bias[q : q + 1] for q in range(blocks)], axis=1)
    for i in range(tiles):
        win = bases[0, i * rows : i * rows + rows + EDGE, :]
        x = window_onehot(win, WIN - EDGE - mid, rows, taps)
        if i == 0:
            for copy in copies:
                copy.wait()
        conv = dot_nn(x, m_all[...]) + line
        out[i * rows : (i + 1) * rows, :] = gelu_parts(conv)[1].astype(BF)


def others(place, bases, bias, part, taps, which):
    batch, ext_rows, width = bases.shape
    rows = ext_rows - 2 * (WIN - EDGE)
    count, blocks, slab, chan = part.shape
    return pl.pallas_call(
        functools.partial(
            others_kernel, tiles=row_tiles(rows), taps=taps, pieces=count
        ),
        grid_spec=pltpu.PrefetchScalarGridSpec(
            num_scalar_prefetch=1,
            grid=(1,),
            in_specs=[
                pl.BlockSpec((1, ext_rows, width), lambda s, p: (which, 0, 0)),
                pl.BlockSpec(bias.shape, lambda s, p: (0, 0)),
            ]
            + [pl.BlockSpec(memory_space=pl.ANY)],
            out_specs=pl.BlockSpec((rows, blocks * chan), lambda s, p: (0, 0)),
            scratch_shapes=[
                pltpu.VMEM((count * slab, blocks * chan), BF),
                pltpu.SemaphoreType.DMA((count, blocks)),
            ],
        ),
        out_shape=jax.ShapeDtypeStruct((rows, blocks * chan), BF),
        compiler_params=params(16),
        cost_estimate=pl.CostEstimate(
            flops=2 * rows * count * slab * blocks * chan,
            bytes_accessed=14_000_000,
            transcendentals=0,
        ),
        name="others",
    )(place, bases, bias, part)


def pair_kernel(row, col, mask, pw, cot, row_out, sum_out, row_t, col_t, row_acc, *, batch):
    s, step = pl.program_id(0), pl.program_id(1)
    steps = pl.num_programs(1)
    many, wide, chan = cot.shape[1], cot.shape[2], cot.shape[3]
    pair_rows = row.shape[1]

    @pl.when(step == 0)
    def _():
        row_t[...] = row[0].T
        col_t[...] = col[0].T
        row_acc[...] = jnp.zeros_like(row_acc)
        sum_out[pl.ds(s, 1)] = jnp.zeros((1,) + sum_out.shape[1:], F32)

    @pl.when((step == 0) & (s == 0))
    def _():
        sum_out[batch] = jnp.zeros(sum_out.shape[1:], F32)

    lane = lax.broadcasted_iota(jnp.int32, (chan, pair_rows), 1)
    keep = mask[...].astype(F32)
    rows_now = row_t[...]
    acts, backs = [], []
    flat = cot[0].reshape(many * wide, chan)
    back = dot_nt(pw[...], flat)
    total = jnp.zeros((chan, wide), F32)
    row_sum = row_acc[...]
    for i in range(many):
        here = lane == step * many + i
        one = jnp.sum(jnp.where(here, rows_now, 0.0), axis=1, keepdims=True)
        pre = col_t[...] + one
        act, slope = gelu_parts(pre)
        line = keep[i : i + 1]
        acts.append((act * line).astype(BF))
        grad = back[:, i * wide : (i + 1) * wide] * (slope * line)
        total = total + grad
        row_sum = row_sum + jnp.where(here, jnp.sum(grad, axis=1, keepdims=True), 0.0)
    row_acc[...] = row_sum
    sum_out[pl.ds(s, 1)] += total[None]
    sum_out[batch] += dot_nn(jnp.concatenate(acts, axis=1), flat)

    @pl.when(step == steps - 1)
    def _():
        row_out[0] = row_acc[...].T
        sum_out[pl.ds(s, 1)] = sum_out[pl.ds(s, 1)].reshape(sum_out.shape[1:]).T[None]


def pair(row, col, mask, pw, cot):
    batch, rows, cols, chan = cot.shape
    many = 16
    return pl.pallas_call(
        functools.partial(pair_kernel, batch=batch),
        grid=(batch, rows // many),
        in_specs=[
            pl.BlockSpec((1, rows, chan), lambda s, i: (s, 0, 0)),
            pl.BlockSpec((1, cols, chan), lambda s, i: (s, 0, 0)),
            pl.BlockSpec((many, cols), lambda s, i: (i, 0)),
            pl.BlockSpec(pw.shape, lambda s, i: (0, 0)),
            pl.BlockSpec((1, many, cols, chan), lambda s, i: (s, i, 0, 0)),
        ],
        out_specs=[
            pl.BlockSpec((1, rows, chan), lambda s, i: (s, 0, 0)),
            pl.BlockSpec((batch + 1, cols, chan), lambda s, i: (0, 0, 0)),
        ],
        out_shape=[
            jax.ShapeDtypeStruct((batch, rows, chan), F32),
            jax.ShapeDtypeStruct((batch + 1, cols, chan), F32),
        ],
        scratch_shapes=[
            pltpu.VMEM((chan, rows), F32),
            pltpu.VMEM((chan, cols), F32),
            pltpu.VMEM((chan, rows), F32),
        ],
        compiler_params=params(8),
        cost_estimate=pl.CostEstimate(
            flops=30 * batch * rows * cols * chan * 16, bytes_accessed=5_000_000, transcendentals=0
        ),
        name="pair",
    )(row, col, mask, pw, cot)


def hot_grad_kernel(place, bases, both, proj, *refs, taps, pool):
    slopes, keep, give, acc = refs[:-3], *refs[-3:]
    rows = slopes[0].shape[0] - 2 * EDGE
    mid = taps // 2
    inner = EDGE // pool
    for s, slope in enumerate(slopes):
        pg = dot_split(both[s], proj[...], dot_nt) * (1.0 / pool)
        pg = spread(pg[inner : inner + rows // pool], pool)
        grad = (slope[EDGE : EDGE + rows, :].astype(F32) * pg).astype(BF)
        x = window_onehot(bases[s, EDGE : EDGE + rows + EDGE, :], WIN - EDGE - mid, rows, taps)
        part = dot_tn(grad, x)
        if s == 0:
            acc[...] = part
        else:
            acc[...] += part
    half = keep.shape[0]
    mine = pl.multiple_of(place[1] * half, 16)
    keep[...] = acc[pl.ds(mine, half), :]
    give[...] = acc[pl.ds(pl.multiple_of(half - mine, 16), half), :].astype(BF)


def hot_grad(place, bases, both, proj, slopes, taps, pool):
    width = bases.shape[2]
    rows, chan = slopes[0].shape
    wide = taps * width * 4
    in_vmem = pl.BlockSpec(memory_space=pltpu.VMEM)
    return pl.pallas_call(
        functools.partial(hot_grad_kernel, taps=taps, pool=pool),
        in_specs=[pl.BlockSpec(memory_space=pltpu.SMEM)] + [in_vmem] * (3 + len(slopes)),
        out_specs=[in_vmem, in_vmem],
        out_shape=[
            jax.ShapeDtypeStruct((chan // 2, wide), F32),
            jax.ShapeDtypeStruct((chan // 2, wide), BF),
        ],
        scratch_shapes=[pltpu.VMEM((chan, wide), F32)],
        compiler_params=params(24),
        cost_estimate=pl.CostEstimate(
            flops=2 * len(slopes) * rows * wide * chan, bytes_accessed=6_000_000, transcendentals=0
        ),
        name="hot_grad",
    )(place, bases, both, proj, *slopes)


def unfold_kernel(place, mine, other, stem, out, hot, *, taps, steps):
    bits = stem.shape[0]
    rows = mine.shape[0]
    piece = rows >> len(steps)
    value = jnp.where(pl.program_id(0) == 0, mine[...], other[...])
    for r in range(rows // piece):
        first = 0
        for at, step in enumerate(steps):
            own = lax.rem(place[2] // step, 2)
            away = (r >> (len(steps) - 1 - at)) & 1
            first = first + (own ^ away) * (rows >> (at + 1))
        here = pl.ds(pl.multiple_of(first, 16), piece)
        hot[here, :] = value[r * piece : (r + 1) * piece]
    for t in range(taps):
        out[t] = dot_nn(hot[:, t * bits : (t + 1) * bits], stem[...]).astype(BF)


def unfold(place, parts, stem, taps):
    rows, wide = parts[0].shape
    bits, full = stem.shape
    steps = powers(lax.axis_size("seq"))[1:]
    return pl.pallas_call(
        functools.partial(unfold_kernel, taps=taps, steps=steps),
        grid_spec=pltpu.PrefetchScalarGridSpec(
            num_scalar_prefetch=1,
            grid=(2,),
            in_specs=[pl.BlockSpec((rows, wide), lambda h, p: (0, 0))] * 2
            + [pl.BlockSpec((bits, full), lambda h, p: (0, 0))],
            out_specs=pl.BlockSpec((taps, rows, full), lambda h, p: (0, p[1] ^ h, 0)),
            scratch_shapes=[pltpu.VMEM((rows, wide), BF)],
        ),
        out_shape=jax.ShapeDtypeStruct((taps, 2 * rows, full), BF),
        compiler_params=params(12),
        cost_estimate=pl.CostEstimate(
            flops=4 * taps * rows * bits * full, bytes_accessed=9_000_000, transcendentals=0
        ),
        name="unfold",
    )(place, *parts, stem)


def token_kernel(place, both, slope, slopes, *refs, cols, pieces, taps, pool, tiles):
    w_other, w_own, proj_own = refs[:3]
    out, w_all, grads, y, sems = refs[-5:]
    ext, chan = slope.shape
    rows = ext - 2 * EDGE
    mid = taps // 2
    slab = chan // pieces
    width = taps * chan
    firsts, copies = [], []
    for t in range(taps):
        copies.append(
            pltpu.make_async_copy(
                w_own.at[t, :, pl.ds(pl.multiple_of(place[0] * chan, 128), chan)],
                w_all.at[0:chan, t * chan : (t + 1) * chan],
                sems.at[pieces, t],
            )
        )
    for r in range(pieces):
        for q in range(1, cols):
            to = q * chan + r * slab
            for group, lanes, at in ((firsts, slice(width, None), 0), (copies, slice(0, width), 1)):
                group.append(
                    pltpu.make_async_copy(
                        w_other.at[r, q - 1, :, lanes],
                        w_all.at[to : to + slab, lanes],
                        sems.at[r, 2 * q + at],
                    )
                )
    for copy in firsts + copies:
        copy.start()
    for copy in firsts:
        copy.wait()

    own = None
    for q in range(cols):
        lanes = slice(q * chan, (q + 1) * chan)
        proj = proj_own[...] if q == 0 else w_all[lanes, width:]
        pg = spread(dot_split(both[0], proj, dot_nt) * (1.0 / pool), pool)
        if q == 0:
            own = pg[EDGE : EDGE + rows]
            now = slope[...]
        else:
            now = slopes[:, (q - 1) * chan : q * chan]
        grads[:, lanes] = (now.astype(F32) * pg).astype(BF)
    for copy in copies:
        copy.wait()
    step = ext // tiles
    for i in range(tiles):
        y[i * step : (i + 1) * step, :] = dot_nn(
            grads[i * step : (i + 1) * step, :], w_all[:, 0:width]
        )
    step = 128
    for i in range(0, rows, step):
        total = own[i : i + step]
        for t in range(taps):
            at = EDGE + mid - t + i
            total = total + y[at : at + step, t * chan : (t + 1) * chan]
        out[0, i : i + step, :] = total.astype(BF)


def token(place, both, slope, slopes, w_other, w_own, proj_own, pool, which, done):
    ext, chan = slope.shape
    taps = w_own.shape[0]
    cols = slopes.shape[1] // chan + 1
    rows = ext - 2 * EDGE
    whole = lambda s, p: (0, 0)
    here = lambda s, p: (which, 0, 0)
    batch = both.shape[0]
    anywhere = pl.BlockSpec(memory_space=pl.ANY)
    into = [] if done is None else [done]
    return pl.pallas_call(
        functools.partial(
            token_kernel, cols=cols, pieces=w_other.shape[0], taps=taps, pool=pool, tiles=row_tiles(ext)
        ),
        grid_spec=pltpu.PrefetchScalarGridSpec(
            num_scalar_prefetch=1,
            grid=(1,),
            in_specs=[
                pl.BlockSpec((1,) + both.shape[1:], here),
                pl.BlockSpec(slope.shape, whole),
                pl.BlockSpec(slopes.shape, whole),
                anywhere,
                anywhere,
                pl.BlockSpec(proj_own.shape, whole),
                *[anywhere for _ in into],
            ],
            out_specs=pl.BlockSpec((1, rows, chan), here),
            scratch_shapes=[
                pltpu.VMEM((cols * chan, w_other.shape[-1]), BF),
                pltpu.VMEM((ext, cols * chan), BF),
                pltpu.VMEM((ext, taps * chan), F32),
                pltpu.SemaphoreType.DMA((w_other.shape[0] + 1, max(taps, 2 * cols))),
            ],
        ),
        out_shape=jax.ShapeDtypeStruct((batch, rows, chan), BF),
        compiler_params=params(24),
        cost_estimate=pl.CostEstimate(
            flops=2 * ext * cols * chan * taps * chan, bytes_accessed=8_000_000, transcendentals=0
        ),
        input_output_aliases={7: 0} if into else {},
        name="token",
    )(place, both, slope, slopes, w_other, w_own, proj_own, *into)


def extended(block, sides, width):
    for axis, dim in sides:
        count = lax.axis_size(axis)
        forward = [(i, i + 1) for i in range(count - 1)]
        backward = [(target, source) for source, target in forward]
        low = lax.ppermute(
            lax.slice_in_dim(block, block.shape[dim] - width, None, axis=dim), axis, forward
        )
        high = lax.ppermute(lax.slice_in_dim(block, 0, width, axis=dim), axis, backward)
        block = jnp.concatenate([low, block, high], axis=dim)
    return block


def gelu_slope(values):
    return jax.vjp(jax.nn.gelu, values)[1](jnp.ones_like(values))[0]


def plain_device(
    bases, stem_weight, conv_weight, conv_bias, pair_proj, pair_weight, pair_cotangent, pair_mask
):
    batch, tok_rows, width_bp = bases.shape
    kernel = conv_weight.shape[0]
    chan_local = conv_weight.shape[1]
    pair_rows = pair_cotangent.shape[1]
    pair_cols = pair_cotangent.shape[2]
    pair_chan = pair_weight.shape[0]
    pool_len = tok_rows // pair_rows
    levels = jnp.arange(4, dtype=jnp.int32)
    onehot = (
        (bases[..., None] == levels).astype(jnp.bfloat16).reshape(batch, tok_rows, width_bp * 4)
    )
    embedded = jnp.einsum(
        "bik,kc->bic", onehot, stem_weight, preferred_element_type=jnp.float32
    ).astype(jnp.bfloat16)
    padded = extended(embedded, (("seq", 1),), 2)
    full_in = lax.all_gather(padded, "col", axis=2, tiled=True)
    conv_out = conv_bias[None, None, :]
    for tap in range(kernel):
        conv_out = conv_out + jnp.einsum(
            "bic,oc->bio",
            full_in[:, tap : tap + tok_rows],
            conv_weight[tap],
            preferred_element_type=jnp.float32,
        )
    features = (embedded.astype(jnp.float32) + jax.nn.gelu(conv_out)).astype(jnp.bfloat16)
    pooled = features.astype(jnp.float32).reshape(batch, pair_rows, pool_len, chan_local).mean(2)
    proj_f = pair_proj.astype(jnp.float32)
    proj_part = jnp.einsum("bmc,cp->bmp", pooled, proj_f, precision=lax.Precision.HIGHEST)
    projected = lax.psum(proj_part, "col")
    row_feat = projected[..., :pair_chan]
    col_own = projected[..., pair_chan:]
    col_every = lax.all_gather(col_own, "seq", axis=1, tiled=True)
    col_feat = lax.dynamic_slice_in_dim(col_every, lax.axis_index("col") * pair_cols, pair_cols, 1)
    pre_act = row_feat[:, :, None, :] + col_feat[:, None, :, :]
    activ = jax.nn.gelu(pre_act).astype(jnp.bfloat16)
    masked = pair_cotangent * pair_mask[None, :, :, None].astype(jnp.bfloat16)
    wgrad_part = jnp.einsum("bmnp,bmnq->pq", activ, masked, preferred_element_type=jnp.float32)
    pair_weight_grad = lax.psum(wgrad_part, ("seq", "col"))
    back = jnp.einsum("bmnq,pq->bmnp", masked, pair_weight, preferred_element_type=jnp.float32)
    pre_grad = back * gelu_slope(pre_act)
    row_grad = lax.psum(pre_grad.sum(2), "col")
    col_block = lax.psum(pre_grad.sum(1), "seq")
    col_whole = lax.all_gather(col_block, "col", axis=1, tiled=True)
    col_grad = lax.dynamic_slice_in_dim(col_whole, lax.axis_index("seq") * pair_rows, pair_rows, 1)
    both_grad = jnp.concatenate([row_grad, col_grad], axis=-1)
    pooled_grad = jnp.einsum("bmp,cp->bmc", both_grad, proj_f, precision=lax.Precision.HIGHEST)
    feat_grad = jnp.repeat(pooled_grad, pool_len, axis=1) / pool_len
    conv_grad = (feat_grad * gelu_slope(conv_out)).astype(jnp.bfloat16)
    weight_part = jnp.stack(
        [
            jnp.einsum(
                "bio,bic->oc",
                conv_grad,
                full_in[:, tap : tap + tok_rows],
                preferred_element_type=jnp.float32,
            )
            for tap in range(kernel)
        ]
    )
    conv_weight_grad = lax.psum(weight_part, "seq").astype(jnp.bfloat16)
    grad_pad = extended(conv_grad, (("seq", 1),), 2)
    turned = lax.all_to_all(conv_weight, "col", split_axis=2, concat_axis=1, tiled=True)
    empty = jnp.zeros((batch, tok_rows, chan_local), jnp.float32)
    total = empty
    piece = lax.all_gather(grad_pad, "col", axis=2, tiled=True)
    for tap in range(kernel):
        total = total + jnp.einsum(
            "bjo,oc->bjc",
            piece[:, 4 - tap : 4 - tap + tok_rows],
            turned[tap],
            preferred_element_type=jnp.float32,
        )
    token_grad = (feat_grad + total).astype(jnp.bfloat16)
    return (token_grad, conv_weight_grad, pair_weight_grad)


def per_device(
    bases, stem_weight, conv_weight, conv_bias, pair_proj, pair_weight, pair_cotangent, pair_mask
):
    batch, tok_rows, width = bases.shape
    taps, chan, full = conv_weight.shape
    pair_rows, pair_cols = pair_cotangent.shape[1:3]
    pair_chan = pair_weight.shape[0]
    pool = tok_rows // pair_rows
    bits = stem_weight.shape[0]
    ns, nc = lax.axis_size("seq"), lax.axis_size("col")
    if chan % 128 or pair_cols % 128 or (chan // ns) % 16 or nc != 4 or batch != 2:
        return plain_device(
            bases, stem_weight, conv_weight, conv_bias, pair_proj, pair_weight, pair_cotangent,
            pair_mask,
        )
    a, b = lax.axis_index("seq"), lax.axis_index("col")
    core = lax.rem(a, 2)
    order, spots = ring_order(nc), ring_spots(nc)
    pick = lambda table: sum(jnp.where(b == i, v, 0) for i, v in enumerate(table))
    place = jnp.stack([b, core, a, pick(spots)]).astype(jnp.int32)
    near = [r for r in range(2, ns, 2) if r & (r - 1) == 0]
    far = [r for r in range(2, ns, 2) if r & (r - 1) != 0]
    odd = list(range(1, ns, 2))
    seq_steps = powers(ns)
    join = lax.optimization_barrier

    def up(x):
        return lax.ppermute(x, "seq", [(i, i + 1) for i in range(ns - 1)])

    def down(x):
        return lax.ppermute(x, "seq", [(i + 1, i) for i in range(ns - 1)])

    def ring(x, k):
        return lax.ppermute(x, "col", [(order[i], order[(i + k) % nc]) for i in range(nc)])

    def slabs(part, chosen):
        for r in chosen:
            low_bit = r & -r
            part[r] = lax.ppermute(part[r - low_bit], "seq", xor_pairs(ns, low_bit))
        return [part[r] for r in chosen]

    def put(part, chosen, values):
        part.update(zip(chosen, values))

    half = lax.dynamic_slice_in_dim(stem_weight, core * (bits // 2), bits // 2, 0)
    mine = [ring(half, k) for k in range(1, nc)]
    marked = bases + 1
    ends = [up(marked[:, tok_rows - WIN :]), down(marked[:, :WIN])]
    slab = chan // ns
    rows_now = lax.dynamic_slice_in_dim(conv_weight, a * slab, slab, 1)
    proj_now = lax.dynamic_slice_in_dim(pair_proj, a * slab, slab, 0)
    blocks = []
    for k in range(1, nc):
        to = pick([order[(spots[i] + k) % nc] for i in range(nc)])
        block = lax.dynamic_slice_in_dim(rows_now, to * chan, chan, 2)
        blocks.append(jnp.concatenate([block[t] for t in range(taps)] + [proj_now], axis=1))
    ext = jnp.concatenate([ends[0], marked, ends[1]], axis=1)
    mine, ext, blocks = join((mine, ext, blocks))
    mine = jnp.stack(mine)

    hi = conv_bias.astype(BF)
    rest = conv_bias - hi.astype(F32)
    mid = rest.astype(BF)
    low = (rest - mid.astype(F32)).astype(BF)
    tail = jnp.concatenate([jnp.stack([hi, mid, low]), jnp.zeros((13, chan), BF)])

    other = lax.ppermute(mine, "seq", xor_pairs(ns, 1))
    turned = [ring(block, k) for k, block in enumerate(blocks, 1)]
    stem, stem_own, m = join(fold(place, stem_weight, mine, other, conv_weight))

    bias = conv_bias[None]
    slope0, proj0 = forward(ext, m, stem_own, bias, pair_proj, taps, pool, 0)
    slope1, proj1 = forward(ext, m, stem_own, bias, pair_proj, taps, pool, 1)
    slope0, slope1, proj0, proj1, turned, m = join((slope0, slope1, proj0, proj1, turned, m))
    turned = lax.all_gather(jnp.stack(turned), "seq", axis=0)

    projected = swap_add(jnp.stack([proj0, proj1]), "col", 1)
    projected, m = join((sum_over(projected, "col", 1), m))
    m_slab = taps * bits // ns
    mine_m = jnp.concatenate([lax.dynamic_slice_in_dim(m, a * m_slab, m_slab, 0), tail])
    part = [ring(mine_m, k) for k in range(1, nc)]
    row_feat = projected[..., :pair_chan]
    col_own = projected[..., pair_chan:]
    wide = jnp.pad(col_own, ((0, 0), (pair_cols, pair_cols), (0, 0)))
    at = jnp.clip(pair_cols - (a * pair_rows - b * pair_cols), 0, pair_cols + pair_rows)
    col_feat = sum_over(lax.dynamic_slice_in_dim(wide, at, pair_cols, 1), "seq")
    row_feat, col_feat = join((row_feat, col_feat))

    row_part, sums = pair(row_feat, col_feat, pair_mask, pair_weight, pair_cotangent)
    row_part, sums, part = join((row_part, sums, part))
    biases = jnp.stack([one[m_slab : m_slab + 3].astype(F32).sum(0) for one in part])
    part = lax.all_gather(jnp.stack([one[:m_slab] for one in part]), "seq", axis=0)

    row_grad = swap_add(row_part, "col", 1)
    sums = join(swap_add(sums, "seq", seq_steps[0]))
    sums, row_grad = join((swap_add(sums, "seq", seq_steps[1]), row_grad))
    row_grad = sum_over(row_grad, "col", 1)
    for step in seq_steps[2:]:
        sums = swap_add(sums, "seq", step)
    sums, row_grad = join((sums, row_grad))
    row_ends = [up(row_grad[:, pair_rows - 1 :]), down(row_grad[:, :1])]
    sums = sums.reshape(-1, pair_chan)
    col_block = sums[: batch * pair_cols].reshape(batch, pair_cols, pair_chan)
    need = pair_rows + 2
    wide = jnp.pad(col_block, ((0, 0), (need, need), (0, 0)))
    at = jnp.clip(a * pair_rows - 1 - b * pair_cols + need, 0, pair_cols + need)
    col_now = lax.dynamic_slice_in_dim(wide, at, need, 1).reshape(batch * need, pair_chan)
    last = sum_over(jnp.concatenate([sums[batch * pair_cols :], col_now]), "col")
    pair_weight_grad = last[:pair_chan]
    row_ext = jnp.concatenate([row_ends[0], row_grad, row_ends[1]], axis=1)
    col_ext = last[pair_chan:].reshape(batch, need, pair_chan)
    both = jnp.concatenate([row_ext, col_ext], axis=-1)
    both = join(both)

    hot_part = hot_grad(place, ext, both, pair_proj, [slope0, slope1], taps, pool)
    hot_part, both, turned, part = join((hot_part, both, turned, part))

    def slopes_of(s):
        return lambda done: (done and done[0], others(place, ext, biases, part, taps, s))

    def tokens(s):
        slope = (slope0, slope1)[s]
        return lambda done: (
            token(place, both, slope, done[1], turned, conv_weight, pair_proj, pool, s, done[0]),
            None,
        )

    beside = [slopes_of(0), tokens(0), slopes_of(1), tokens(1)]
    hot_sum, token_grad = reduce_hot(hot_part, a, ns, beside)
    conv_weight_grad = unfold(place, hot_sum, stem, taps)
    return (token_grad, conv_weight_grad, pair_weight_grad)


def reduce_hot(x, a, ns, beside):
    steps = powers(ns)
    join = lax.optimization_barrier

    def swap(v, step):
        return lax.ppermute(v, "seq", xor_pairs(ns, step))

    keep, give = x
    x = keep + swap(give, steps[0]).astype(F32)
    done = None
    for at, step in enumerate(steps[1:]):
        size = x.shape[0] // 2
        bit = lax.rem(a // step, 2)
        keep = lax.dynamic_slice_in_dim(x, bit * size, size, 0)
        give = lax.dynamic_slice_in_dim(x, (1 - bit) * size, size, 0).astype(BF)
        keep, give, done = join((keep, give, done))
        got = swap(give, step)
        if at < len(beside):
            done = beside[at](done)
        keep, got, done = join((keep, got, done))
        x = keep + got.astype(F32)
    x = x.astype(BF)
    for at, step in enumerate(steps[:0:-1], len(steps) - 1):
        x, done = join((x, done))
        got = swap(x, step)
        if at < len(beside):
            done = beside[at](done)
        x, got, done = join((x, got, done))
        x = jnp.concatenate([x, got])
    return [x, swap(x, steps[0])], done[0]


def solution(mesh):
    placed = (
        P(None, "seq", None),
        P(None, "col"),
        P(None, "col", None),
        P("col"),
        P("col", None),
        P(),
        P(None, "seq", "col", None),
        P("seq", "col"),
    )
    return jax.shard_map(
        per_device,
        mesh=mesh,
        in_specs=placed,
        out_specs=(P(None, "seq", "col"), P(None, "col", None), P()),
        check_vma=False,
    )
```

```python
import functools

import jax
import jax.numpy as jnp
from jax import lax
from jax.experimental import pallas as pl
from jax.experimental.pallas import tpu as pltpu
from jax.sharding import PartitionSpec as P

BF, F32 = jnp.bfloat16, jnp.float32
EDGE = 16
WIN = 24
ROOT = 0.7978845608028654
CUBE = 0.044715


def gelu_parts(x):
    sq = x * x
    th = jnp.tanh(x * (ROOT + (ROOT * CUBE) * sq))
    half = 0.5 + 0.5 * th
    act = x * half
    return act, half + act * (1.0 - th) * (ROOT + (3.0 * ROOT * CUBE) * sq)


def dot_nn(a, b):
    return lax.dot_general(a, b, (((1,), (0,)), ((), ())), preferred_element_type=F32)


def dot_nt(a, b):
    return lax.dot_general(a, b, (((1,), (1,)), ((), ())), preferred_element_type=F32)


def dot_tn(a, b):
    return lax.dot_general(a, b, (((0,), (0,)), ((), ())), preferred_element_type=F32)


def dot_split(a, b, dot):
    hi = a.astype(BF)
    rest = a - hi.astype(F32)
    mid = rest.astype(BF)
    low = (rest - mid.astype(F32)).astype(BF)
    return dot(hi, b) + dot(mid, b) + dot(low, b)


def xor_pairs(count, step):
    return [(i, i ^ step) for i in range(count)]


def sum_over(x, axis, first=0):
    for step in powers(lax.axis_size(axis))[first:]:
        x = swap_add(x, axis, step)
    return x


def after(x, *earlier):
    return lax.optimization_barrier((x,) + earlier)[0]


def swap_add(x, axis, step):
    return x + lax.ppermute(x, axis, xor_pairs(lax.axis_size(axis), step))


def powers(count):
    steps = [1]
    while 2 * steps[-1] < count:
        steps.append(2 * steps[-1])
    return steps


def ring_order(count):
    return list(range(0, count, 2)) + list(range(1, count, 2))[::-1]


def ring_spots(count):
    order = ring_order(count)
    return [order.index(i) for i in range(count)]


def window_onehot(win, first, rows, taps, levels=4):
    parts = []
    for tap in range(taps):
        own = win[first + tap : first + tap + rows]
        for level in range(levels):
            parts.append(jnp.where(own == level + 1, 1.0, 0.0).astype(BF))
    return jnp.concatenate(parts, axis=1)


def spread(pg, pool):
    groups, chan = pg.shape
    return jnp.broadcast_to(pg[:, None, :], (groups, pool, chan)).reshape(groups * pool, chan)


def params(mebibytes):
    return pltpu.CompilerParams(vmem_limit_bytes=mebibytes * 1024 * 1024)


def fold_kernel(place, own, mine, other, w, stem_out, own_out, m_out, *, cols, spots):
    bits, chan = own.shape
    half = bits // 2
    per = bits // 4

    @pl.when(pl.program_id(0) == 0)
    def _():
        c = place[1]

        def pick(width, base):
            dst = lax.broadcasted_iota(jnp.int32, (bits, width), 0)
            src = 4 * (dst & (per - 1)) + (dst >> (per.bit_length() - 1))
            at = lax.broadcasted_iota(jnp.int32, (bits, width), 1) + base
            return jnp.where(src == at, 1.0, 0.0).astype(BF)

        own_p = dot_nn(pick(bits, 0), own[...]).astype(BF)
        own_out[...] = own_p
        pick_mine, pick_other = pick(half, half * c), pick(half, half * (1 - c))
        for j in range(cols):
            k = lax.rem(place[3] - spots[j] + cols, cols)
            at = jnp.maximum(k - 1, 0)
            got = dot_nn(pick_mine, mine[at]) + dot_nn(pick_other, other[at])
            stem_out[:, j * chan : (j + 1) * chan] = jnp.where(k == 0, own_p, got.astype(BF))

    m_out[...] = dot_nt(stem_out[...], w[0]).astype(BF)


def fold(place, own, mine, other, weight):
    taps, chan, full = weight.shape
    bits = own.shape[0]
    cols = full // chan
    whole = lambda t, p: (0, 0)
    whole3 = lambda t, p: (0, 0, 0)
    return pl.pallas_call(
        functools.partial(fold_kernel, cols=cols, spots=ring_spots(cols)),
        grid_spec=pltpu.PrefetchScalarGridSpec(
            num_scalar_prefetch=1,
            grid=(taps,),
            in_specs=[
                pl.BlockSpec(own.shape, whole),
                pl.BlockSpec(mine.shape, whole3),
                pl.BlockSpec(other.shape, whole3),
                pl.BlockSpec((1, chan, full), lambda t, p: (t, 0, 0)),
            ],
            out_specs=[
                pl.BlockSpec((bits, full), whole),
                pl.BlockSpec((bits, chan), whole),
                pl.BlockSpec((bits, chan), lambda t, p: (t, 0)),
            ],
        ),
        out_shape=[
            jax.ShapeDtypeStruct((bits, full), BF),
            jax.ShapeDtypeStruct((bits, chan), BF),
            jax.ShapeDtypeStruct((taps * bits, chan), BF),
        ],
        compiler_params=params(10),
        cost_estimate=pl.CostEstimate(
            flops=2 * taps * bits * chan * full, bytes_accessed=8_000_000, transcendentals=0
        ),
        name="fold",
    )(place, own, mine, other, weight)


def forward_kernel(bases, m, stem, bias, proj, slope_out, proj_out, *, tiles, taps, pool):
    rows = slope_out.shape[1] // tiles
    bits = stem.shape[0]
    mid = taps // 2
    pooled = []
    for i in range(tiles):
        win = bases[0, i * rows : i * rows + rows + EDGE, :]
        x = window_onehot(win, WIN - EDGE - mid, rows, taps)
        conv = dot_nn(x, m[...]) + bias[...]
        embedded = dot_nn(x[:, mid * bits : (mid + 1) * bits], stem[...]).astype(BF)
        act, slope = gelu_parts(conv)
        slope_out[0, i * rows : (i + 1) * rows, :] = slope.astype(BF)
        feats = (embedded.astype(F32) + act).astype(BF).astype(F32)
        pooled.append(feats.reshape(rows // pool, pool, feats.shape[1]).sum(1))
    pooled = jnp.concatenate(pooled, axis=0)
    inner = EDGE // pool
    pooled = pooled[inner : inner + proj_out.shape[1]] * (1.0 / pool)
    proj_out[0] = dot_split(pooled, proj[...], dot_nn)


def row_tiles(rows):
    for tiles in range(1, rows + 1):
        if rows % (tiles * 16) == 0 and rows // tiles <= 352:
            return tiles
    return 1


def forward(bases, m, stem, bias, proj, taps, pool):
    batch, ext_rows, width = bases.shape
    rows = ext_rows - 2 * (WIN - EDGE)
    chan = stem.shape[1]
    pairs = (rows - 2 * EDGE) // pool
    two = lambda s: (0, 0)
    return pl.pallas_call(
        functools.partial(forward_kernel, tiles=row_tiles(rows), taps=taps, pool=pool),
        grid=(batch,),
        in_specs=[
            pl.BlockSpec((1, ext_rows, width), lambda s: (s, 0, 0)),
            pl.BlockSpec(m.shape, two),
            pl.BlockSpec(stem.shape, two),
            pl.BlockSpec(bias.shape, two),
            pl.BlockSpec(proj.shape, two),
        ],
        out_specs=[
            pl.BlockSpec((1, rows, chan), lambda s: (s, 0, 0)),
            pl.BlockSpec((1, pairs, proj.shape[1]), lambda s: (s, 0, 0)),
        ],
        out_shape=[
            jax.ShapeDtypeStruct((batch, rows, chan), BF),
            jax.ShapeDtypeStruct((batch, pairs, proj.shape[1]), F32),
        ],
        compiler_params=params(10),
        cost_estimate=pl.CostEstimate(
            flops=2 * batch * rows * m.shape[0] * chan, bytes_accessed=6_000_000, transcendentals=0
        ),
        name="forward",
    )(bases, m, stem, bias, proj)


def others_kernel(place, bases, bias, *refs, tiles, taps, pieces):
    part, out, m_all, sems = refs
    _, blocks, slab, chan = part.shape
    rows = out.shape[0] // tiles
    mid = taps // 2

    copies = []
    for r in range(pieces):
        for q in range(blocks):
            copies.append(
                pltpu.make_async_copy(
                    part.at[r, q],
                    m_all.at[r * slab : (r + 1) * slab, q * chan : (q + 1) * chan],
                    sems.at[r, q],
                )
            )
    for copy in copies:
        copy.start()

    line = jnp.concatenate([bias[q : q + 1] for q in range(blocks)], axis=1)
    for i in range(tiles):
        win = bases[0, i * rows : i * rows + rows + EDGE, :]
        x = window_onehot(win, WIN - EDGE - mid, rows, taps)
        if i == 0:
            for copy in copies:
                copy.wait()
        conv = dot_nn(x, m_all[...]) + line
        out[i * rows : (i + 1) * rows, :] = gelu_parts(conv)[1].astype(BF)


def others(place, bases, bias, part, taps, which):
    batch, ext_rows, width = bases.shape
    rows = ext_rows - 2 * (WIN - EDGE)
    count, blocks, slab, chan = part.shape
    return pl.pallas_call(
        functools.partial(
            others_kernel, tiles=row_tiles(rows), taps=taps, pieces=count
        ),
        grid_spec=pltpu.PrefetchScalarGridSpec(
            num_scalar_prefetch=1,
            grid=(1,),
            in_specs=[
                pl.BlockSpec((1, ext_rows, width), lambda s, p: (which, 0, 0)),
                pl.BlockSpec(bias.shape, lambda s, p: (0, 0)),
            ]
            + [pl.BlockSpec(memory_space=pl.ANY)],
            out_specs=pl.BlockSpec((rows, blocks * chan), lambda s, p: (0, 0)),
            scratch_shapes=[
                pltpu.VMEM((count * slab, blocks * chan), BF),
                pltpu.SemaphoreType.DMA((count, blocks)),
            ],
        ),
        out_shape=jax.ShapeDtypeStruct((rows, blocks * chan), BF),
        compiler_params=params(16),
        cost_estimate=pl.CostEstimate(
            flops=2 * rows * count * slab * blocks * chan,
            bytes_accessed=14_000_000,
            transcendentals=0,
        ),
        name="others",
    )(place, bases, bias, part)


def pair_kernel(row, col, mask, pw, cot, row_out, sum_out, row_t, col_t, row_acc, *, batch):
    s, step = pl.program_id(0), pl.program_id(1)
    steps = pl.num_programs(1)
    many, wide, chan = cot.shape[1], cot.shape[2], cot.shape[3]
    pair_rows = row.shape[1]

    @pl.when(step == 0)
    def _():
        row_t[...] = row[0].T
        col_t[...] = col[0].T
        row_acc[...] = jnp.zeros_like(row_acc)
        sum_out[pl.ds(s, 1)] = jnp.zeros((1,) + sum_out.shape[1:], F32)

    @pl.when((step == 0) & (s == 0))
    def _():
        sum_out[batch] = jnp.zeros(sum_out.shape[1:], F32)

    lane = lax.broadcasted_iota(jnp.int32, (chan, pair_rows), 1)
    keep = mask[...].astype(F32)
    rows_now = row_t[...]
    acts, backs = [], []
    flat = cot[0].reshape(many * wide, chan)
    back = dot_nt(pw[...], flat)
    total = jnp.zeros((chan, wide), F32)
    row_sum = row_acc[...]
    for i in range(many):
        here = lane == step * many + i
        one = jnp.sum(jnp.where(here, rows_now, 0.0), axis=1, keepdims=True)
        pre = col_t[...] + one
        act, slope = gelu_parts(pre)
        line = keep[i : i + 1]
        acts.append((act * line).astype(BF))
        grad = back[:, i * wide : (i + 1) * wide] * (slope * line)
        total = total + grad
        row_sum = row_sum + jnp.where(here, jnp.sum(grad, axis=1, keepdims=True), 0.0)
    row_acc[...] = row_sum
    sum_out[pl.ds(s, 1)] += total[None]
    sum_out[batch] += dot_nn(jnp.concatenate(acts, axis=1), flat)

    @pl.when(step == steps - 1)
    def _():
        row_out[0] = row_acc[...].T
        sum_out[pl.ds(s, 1)] = sum_out[pl.ds(s, 1)].reshape(sum_out.shape[1:]).T[None]


def pair(row, col, mask, pw, cot):
    batch, rows, cols, chan = cot.shape
    many = 16
    return pl.pallas_call(
        functools.partial(pair_kernel, batch=batch),
        grid=(batch, rows // many),
        in_specs=[
            pl.BlockSpec((1, rows, chan), lambda s, i: (s, 0, 0)),
            pl.BlockSpec((1, cols, chan), lambda s, i: (s, 0, 0)),
            pl.BlockSpec((many, cols), lambda s, i: (i, 0)),
            pl.BlockSpec(pw.shape, lambda s, i: (0, 0)),
            pl.BlockSpec((1, many, cols, chan), lambda s, i: (s, i, 0, 0)),
        ],
        out_specs=[
            pl.BlockSpec((1, rows, chan), lambda s, i: (s, 0, 0)),
            pl.BlockSpec((batch + 1, cols, chan), lambda s, i: (0, 0, 0)),
        ],
        out_shape=[
            jax.ShapeDtypeStruct((batch, rows, chan), F32),
            jax.ShapeDtypeStruct((batch + 1, cols, chan), F32),
        ],
        scratch_shapes=[
            pltpu.VMEM((chan, rows), F32),
            pltpu.VMEM((chan, cols), F32),
            pltpu.VMEM((chan, rows), F32),
        ],
        compiler_params=params(8),
        cost_estimate=pl.CostEstimate(
            flops=30 * batch * rows * cols * chan * 16, bytes_accessed=5_000_000, transcendentals=0
        ),
        name="pair",
    )(row, col, mask, pw, cot)


def hot_grad_kernel(place, bases, both, proj, *refs, taps, pool):
    slopes, keep, give, acc = refs
    rows = slopes.shape[1] - 2 * EDGE
    mid = taps // 2
    inner = EDGE // pool
    for s in range(slopes.shape[0]):
        pg = dot_split(both[s], proj[...], dot_nt) * (1.0 / pool)
        pg = spread(pg[inner : inner + rows // pool], pool)
        grad = (slopes[s, EDGE : EDGE + rows, :].astype(F32) * pg).astype(BF)
        x = window_onehot(bases[s, EDGE : EDGE + rows + EDGE, :], WIN - EDGE - mid, rows, taps)
        part = dot_tn(grad, x)
        if s == 0:
            acc[...] = part
        else:
            acc[...] += part
    half = keep.shape[0]
    mine = pl.multiple_of(place[1] * half, 16)
    keep[...] = acc[pl.ds(mine, half), :]
    give[...] = acc[pl.ds(pl.multiple_of(half - mine, 16), half), :].astype(BF)


def hot_grad(place, bases, both, proj, slopes, taps, pool):
    width = bases.shape[2]
    batch, rows, chan = slopes.shape
    wide = taps * width * 4
    in_vmem = pl.BlockSpec(memory_space=pltpu.VMEM)
    return pl.pallas_call(
        functools.partial(hot_grad_kernel, taps=taps, pool=pool),
        in_specs=[pl.BlockSpec(memory_space=pltpu.SMEM)] + [in_vmem] * 4,
        out_specs=[in_vmem, in_vmem],
        out_shape=[
            jax.ShapeDtypeStruct((chan // 2, wide), F32),
            jax.ShapeDtypeStruct((chan // 2, wide), BF),
        ],
        scratch_shapes=[pltpu.VMEM((chan, wide), F32)],
        compiler_params=params(24),
        cost_estimate=pl.CostEstimate(
            flops=2 * batch * rows * wide * chan, bytes_accessed=6_000_000, transcendentals=0
        ),
        name="hot_grad",
    )(place, bases, both, proj, slopes)


def unfold_kernel(place, mine, other, stem, out, hot, *, taps, steps):
    bits = stem.shape[0]
    rows = mine.shape[0]
    piece = rows >> len(steps)
    value = jnp.where(pl.program_id(0) == 0, mine[...], other[...])
    for r in range(rows // piece):
        first = 0
        for at, step in enumerate(steps):
            own = lax.rem(place[2] // step, 2)
            away = (r >> (len(steps) - 1 - at)) & 1
            first = first + (own ^ away) * (rows >> (at + 1))
        here = pl.ds(pl.multiple_of(first, 16), piece)
        hot[here, :] = value[r * piece : (r + 1) * piece]
    for t in range(taps):
        out[t] = dot_nn(hot[:, t * bits : (t + 1) * bits], stem[...]).astype(BF)


def unfold(place, parts, stem, taps):
    rows, wide = parts[0].shape
    bits, full = stem.shape
    steps = powers(lax.axis_size("seq"))[1:]
    return pl.pallas_call(
        functools.partial(unfold_kernel, taps=taps, steps=steps),
        grid_spec=pltpu.PrefetchScalarGridSpec(
            num_scalar_prefetch=1,
            grid=(2,),
            in_specs=[pl.BlockSpec((rows, wide), lambda h, p: (0, 0))] * 2
            + [pl.BlockSpec((bits, full), lambda h, p: (0, 0))],
            out_specs=pl.BlockSpec((taps, rows, full), lambda h, p: (0, p[1] ^ h, 0)),
            scratch_shapes=[pltpu.VMEM((rows, wide), BF)],
        ),
        out_shape=jax.ShapeDtypeStruct((taps, 2 * rows, full), BF),
        compiler_params=params(12),
        cost_estimate=pl.CostEstimate(
            flops=4 * taps * rows * bits * full, bytes_accessed=9_000_000, transcendentals=0
        ),
        name="unfold",
    )(place, *parts, stem)


def token_kernel(place, both, slope, slopes, *refs, cols, pieces, taps, pool, tiles):
    w_other, w_own, proj_own = refs[:3]
    out, w_all, grads, y, sems = refs[-5:]
    _, ext, chan = slope.shape
    rows = ext - 2 * EDGE
    mid = taps // 2
    slab = chan // pieces
    width = taps * chan
    firsts, copies = [], []
    for t in range(taps):
        copies.append(
            pltpu.make_async_copy(
                w_own.at[t, :, pl.ds(pl.multiple_of(place[0] * chan, 128), chan)],
                w_all.at[0:chan, t * chan : (t + 1) * chan],
                sems.at[pieces, t],
            )
        )
    for r in range(pieces):
        for q in range(1, cols):
            to = q * chan + r * slab
            for group, lanes, at in ((firsts, slice(width, None), 0), (copies, slice(0, width), 1)):
                group.append(
                    pltpu.make_async_copy(
                        w_other.at[r, q - 1, :, lanes],
                        w_all.at[to : to + slab, lanes],
                        sems.at[r, 2 * q + at],
                    )
                )
    for copy in firsts + copies:
        copy.start()
    for copy in firsts:
        copy.wait()

    own = None
    for q in range(cols):
        lanes = slice(q * chan, (q + 1) * chan)
        proj = proj_own[...] if q == 0 else w_all[lanes, width:]
        pg = spread(dot_split(both[0], proj, dot_nt) * (1.0 / pool), pool)
        if q == 0:
            own = pg[EDGE : EDGE + rows]
            now = slope[0]
        else:
            now = slopes[:, (q - 1) * chan : q * chan]
        grads[:, lanes] = (now.astype(F32) * pg).astype(BF)
    for copy in copies:
        copy.wait()
    step = ext // tiles
    for i in range(tiles):
        y[i * step : (i + 1) * step, :] = dot_nn(
            grads[i * step : (i + 1) * step, :], w_all[:, 0:width]
        )
    step = 128
    for i in range(0, rows, step):
        total = own[i : i + step]
        for t in range(taps):
            at = EDGE + mid - t + i
            total = total + y[at : at + step, t * chan : (t + 1) * chan]
        out[0, i : i + step, :] = total.astype(BF)


def token(place, both, slope, slopes, w_other, w_own, proj_own, pool, which, done):
    _, ext, chan = slope.shape
    taps = w_own.shape[0]
    cols = slopes.shape[1] // chan + 1
    rows = ext - 2 * EDGE
    whole = lambda s, p: (0, 0)
    here = lambda s, p: (which, 0, 0)
    batch = both.shape[0]
    anywhere = pl.BlockSpec(memory_space=pl.ANY)
    into = [] if done is None else [done]
    return pl.pallas_call(
        functools.partial(
            token_kernel, cols=cols, pieces=w_other.shape[0], taps=taps, pool=pool, tiles=row_tiles(ext)
        ),
        grid_spec=pltpu.PrefetchScalarGridSpec(
            num_scalar_prefetch=1,
            grid=(1,),
            in_specs=[
                pl.BlockSpec((1,) + both.shape[1:], here),
                pl.BlockSpec((1, ext, chan), here),
                pl.BlockSpec(slopes.shape, whole),
                anywhere,
                anywhere,
                pl.BlockSpec(proj_own.shape, whole),
                *[anywhere for _ in into],
            ],
            out_specs=pl.BlockSpec((1, rows, chan), here),
            scratch_shapes=[
                pltpu.VMEM((cols * chan, w_other.shape[-1]), BF),
                pltpu.VMEM((ext, cols * chan), BF),
                pltpu.VMEM((ext, taps * chan), F32),
                pltpu.SemaphoreType.DMA((w_other.shape[0] + 1, max(taps, 2 * cols))),
            ],
        ),
        out_shape=jax.ShapeDtypeStruct((batch, rows, chan), BF),
        compiler_params=params(24),
        cost_estimate=pl.CostEstimate(
            flops=2 * ext * cols * chan * taps * chan, bytes_accessed=8_000_000, transcendentals=0
        ),
        input_output_aliases={7: 0} if into else {},
        name="token",
    )(place, both, slope, slopes, w_other, w_own, proj_own, *into)


def extended(block, sides, width):
    for axis, dim in sides:
        count = lax.axis_size(axis)
        forward = [(i, i + 1) for i in range(count - 1)]
        backward = [(target, source) for source, target in forward]
        low = lax.ppermute(
            lax.slice_in_dim(block, block.shape[dim] - width, None, axis=dim), axis, forward
        )
        high = lax.ppermute(lax.slice_in_dim(block, 0, width, axis=dim), axis, backward)
        block = jnp.concatenate([low, block, high], axis=dim)
    return block


def gelu_slope(values):
    return jax.vjp(jax.nn.gelu, values)[1](jnp.ones_like(values))[0]


def plain_device(
    bases, stem_weight, conv_weight, conv_bias, pair_proj, pair_weight, pair_cotangent, pair_mask
):
    batch, tok_rows, width_bp = bases.shape
    kernel = conv_weight.shape[0]
    chan_local = conv_weight.shape[1]
    pair_rows = pair_cotangent.shape[1]
    pair_cols = pair_cotangent.shape[2]
    pair_chan = pair_weight.shape[0]
    pool_len = tok_rows // pair_rows
    levels = jnp.arange(4, dtype=jnp.int32)
    onehot = (
        (bases[..., None] == levels).astype(jnp.bfloat16).reshape(batch, tok_rows, width_bp * 4)
    )
    embedded = jnp.einsum(
        "bik,kc->bic", onehot, stem_weight, preferred_element_type=jnp.float32
    ).astype(jnp.bfloat16)
    padded = extended(embedded, (("seq", 1),), 2)
    full_in = lax.all_gather(padded, "col", axis=2, tiled=True)
    conv_out = conv_bias[None, None, :]
    for tap in range(kernel):
        conv_out = conv_out + jnp.einsum(
            "bic,oc->bio",
            full_in[:, tap : tap + tok_rows],
            conv_weight[tap],
            preferred_element_type=jnp.float32,
        )
    features = (embedded.astype(jnp.float32) + jax.nn.gelu(conv_out)).astype(jnp.bfloat16)
    pooled = features.astype(jnp.float32).reshape(batch, pair_rows, pool_len, chan_local).mean(2)
    proj_f = pair_proj.astype(jnp.float32)
    proj_part = jnp.einsum("bmc,cp->bmp", pooled, proj_f, precision=lax.Precision.HIGHEST)
    projected = lax.psum(proj_part, "col")
    row_feat = projected[..., :pair_chan]
    col_own = projected[..., pair_chan:]
    col_every = lax.all_gather(col_own, "seq", axis=1, tiled=True)
    col_feat = lax.dynamic_slice_in_dim(col_every, lax.axis_index("col") * pair_cols, pair_cols, 1)
    pre_act = row_feat[:, :, None, :] + col_feat[:, None, :, :]
    activ = jax.nn.gelu(pre_act).astype(jnp.bfloat16)
    masked = pair_cotangent * pair_mask[None, :, :, None].astype(jnp.bfloat16)
    wgrad_part = jnp.einsum("bmnp,bmnq->pq", activ, masked, preferred_element_type=jnp.float32)
    pair_weight_grad = lax.psum(wgrad_part, ("seq", "col"))
    back = jnp.einsum("bmnq,pq->bmnp", masked, pair_weight, preferred_element_type=jnp.float32)
    pre_grad = back * gelu_slope(pre_act)
    row_grad = lax.psum(pre_grad.sum(2), "col")
    col_block = lax.psum(pre_grad.sum(1), "seq")
    col_whole = lax.all_gather(col_block, "col", axis=1, tiled=True)
    col_grad = lax.dynamic_slice_in_dim(col_whole, lax.axis_index("seq") * pair_rows, pair_rows, 1)
    both_grad = jnp.concatenate([row_grad, col_grad], axis=-1)
    pooled_grad = jnp.einsum("bmp,cp->bmc", both_grad, proj_f, precision=lax.Precision.HIGHEST)
    feat_grad = jnp.repeat(pooled_grad, pool_len, axis=1) / pool_len
    conv_grad = (feat_grad * gelu_slope(conv_out)).astype(jnp.bfloat16)
    weight_part = jnp.stack(
        [
            jnp.einsum(
                "bio,bic->oc",
                conv_grad,
                full_in[:, tap : tap + tok_rows],
                preferred_element_type=jnp.float32,
            )
            for tap in range(kernel)
        ]
    )
    conv_weight_grad = lax.psum(weight_part, "seq").astype(jnp.bfloat16)
    grad_pad = extended(conv_grad, (("seq", 1),), 2)
    turned = lax.all_to_all(conv_weight, "col", split_axis=2, concat_axis=1, tiled=True)
    empty = jnp.zeros((batch, tok_rows, chan_local), jnp.float32)
    total = empty
    piece = lax.all_gather(grad_pad, "col", axis=2, tiled=True)
    for tap in range(kernel):
        total = total + jnp.einsum(
            "bjo,oc->bjc",
            piece[:, 4 - tap : 4 - tap + tok_rows],
            turned[tap],
            preferred_element_type=jnp.float32,
        )
    token_grad = (feat_grad + total).astype(jnp.bfloat16)
    return (token_grad, conv_weight_grad, pair_weight_grad)


def per_device(
    bases, stem_weight, conv_weight, conv_bias, pair_proj, pair_weight, pair_cotangent, pair_mask
):
    batch, tok_rows, width = bases.shape
    taps, chan, full = conv_weight.shape
    pair_rows, pair_cols = pair_cotangent.shape[1:3]
    pair_chan = pair_weight.shape[0]
    pool = tok_rows // pair_rows
    bits = stem_weight.shape[0]
    ns, nc = lax.axis_size("seq"), lax.axis_size("col")
    if chan % 128 or pair_cols % 128 or (chan // ns) % 16 or nc != 4 or batch != 2:
        return plain_device(
            bases, stem_weight, conv_weight, conv_bias, pair_proj, pair_weight, pair_cotangent,
            pair_mask,
        )
    a, b = lax.axis_index("seq"), lax.axis_index("col")
    core = lax.rem(a, 2)
    order, spots = ring_order(nc), ring_spots(nc)
    pick = lambda table: sum(jnp.where(b == i, v, 0) for i, v in enumerate(table))
    place = jnp.stack([b, core, a, pick(spots)]).astype(jnp.int32)
    near = [r for r in range(2, ns, 2) if r & (r - 1) == 0]
    far = [r for r in range(2, ns, 2) if r & (r - 1) != 0]
    odd = list(range(1, ns, 2))
    seq_steps = powers(ns)
    join = lax.optimization_barrier

    def up(x):
        return lax.ppermute(x, "seq", [(i, i + 1) for i in range(ns - 1)])

    def down(x):
        return lax.ppermute(x, "seq", [(i + 1, i) for i in range(ns - 1)])

    def ring(x, k):
        return lax.ppermute(x, "col", [(order[i], order[(i + k) % nc]) for i in range(nc)])

    def slabs(part, chosen):
        for r in chosen:
            low_bit = r & -r
            part[r] = lax.ppermute(part[r - low_bit], "seq", xor_pairs(ns, low_bit))
        return [part[r] for r in chosen]

    def put(part, chosen, values):
        part.update(zip(chosen, values))

    half = lax.dynamic_slice_in_dim(stem_weight, core * (bits // 2), bits // 2, 0)
    mine = [ring(half, k) for k in range(1, nc)]
    marked = bases + 1
    ends = [up(marked[:, tok_rows - WIN :]), down(marked[:, :WIN])]
    slab = chan // ns
    rows_now = lax.dynamic_slice_in_dim(conv_weight, a * slab, slab, 1)
    proj_now = lax.dynamic_slice_in_dim(pair_proj, a * slab, slab, 0)
    blocks = []
    for k in range(1, nc):
        to = pick([order[(spots[i] + k) % nc] for i in range(nc)])
        block = lax.dynamic_slice_in_dim(rows_now, to * chan, chan, 2)
        blocks.append(jnp.concatenate([block[t] for t in range(taps)] + [proj_now], axis=1))
    ext = jnp.concatenate([ends[0], marked, ends[1]], axis=1)
    mine, ext, blocks = join((mine, ext, blocks))
    mine = jnp.stack(mine)

    hi = conv_bias.astype(BF)
    rest = conv_bias - hi.astype(F32)
    mid = rest.astype(BF)
    low = (rest - mid.astype(F32)).astype(BF)
    tail = jnp.concatenate([jnp.stack([hi, mid, low]), jnp.zeros((13, chan), BF)])

    other = lax.ppermute(mine, "seq", xor_pairs(ns, 1))
    turned = [ring(block, k) for k, block in enumerate(blocks, 1)]
    stem, stem_own, m = join(fold(place, stem_weight, mine, other, conv_weight))

    bias = conv_bias[None]
    slope, proj_part = forward(ext, m, stem_own, bias, pair_proj, taps, pool)
    slope, proj_part, turned, m = join((slope, proj_part, turned, m))
    turned = lax.all_gather(jnp.stack(turned), "seq", axis=0)

    projected = swap_add(proj_part, "col", 1)
    projected, m = join((sum_over(projected, "col", 1), m))
    m_slab = taps * bits // ns
    mine_m = jnp.concatenate([lax.dynamic_slice_in_dim(m, a * m_slab, m_slab, 0), tail])
    part = [ring(mine_m, k) for k in range(1, nc)]
    row_feat = projected[..., :pair_chan]
    col_own = projected[..., pair_chan:]
    wide = jnp.pad(col_own, ((0, 0), (pair_cols, pair_cols), (0, 0)))
    at = jnp.clip(pair_cols - (a * pair_rows - b * pair_cols), 0, pair_cols + pair_rows)
    col_feat = sum_over(lax.dynamic_slice_in_dim(wide, at, pair_cols, 1), "seq")
    row_feat, col_feat = join((row_feat, col_feat))

    row_part, sums = pair(row_feat, col_feat, pair_mask, pair_weight, pair_cotangent)
    row_part, sums, part = join((row_part, sums, part))
    biases = jnp.stack([one[m_slab : m_slab + 3].astype(F32).sum(0) for one in part])
    part = lax.all_gather(jnp.stack([one[:m_slab] for one in part]), "seq", axis=0)

    row_grad = swap_add(row_part, "col", 1)
    sums = join(swap_add(sums, "seq", seq_steps[0]))
    sums, row_grad = join((swap_add(sums, "seq", seq_steps[1]), row_grad))
    row_grad = sum_over(row_grad, "col", 1)
    for step in seq_steps[2:]:
        sums = swap_add(sums, "seq", step)
    sums, row_grad = join((sums, row_grad))
    row_ends = [up(row_grad[:, pair_rows - 1 :]), down(row_grad[:, :1])]
    sums = sums.reshape(-1, pair_chan)
    col_block = sums[: batch * pair_cols].reshape(batch, pair_cols, pair_chan)
    need = pair_rows + 2
    wide = jnp.pad(col_block, ((0, 0), (need, need), (0, 0)))
    at = jnp.clip(a * pair_rows - 1 - b * pair_cols + need, 0, pair_cols + need)
    col_now = lax.dynamic_slice_in_dim(wide, at, need, 1).reshape(batch * need, pair_chan)
    last = sum_over(jnp.concatenate([sums[batch * pair_cols :], col_now]), "col")
    pair_weight_grad = last[:pair_chan]
    row_ext = jnp.concatenate([row_ends[0], row_grad, row_ends[1]], axis=1)
    col_ext = last[pair_chan:].reshape(batch, need, pair_chan)
    both = jnp.concatenate([row_ext, col_ext], axis=-1)
    both = join(both)

    hot_part = hot_grad(place, ext, both, pair_proj, slope, taps, pool)
    hot_part, both, turned, part = join((hot_part, both, turned, part))

    def slopes_of(s):
        return lambda done: (done and done[0], others(place, ext, biases, part, taps, s))

    def tokens(s):
        return lambda done: (
            token(place, both, slope, done[1], turned, conv_weight, pair_proj, pool, s, done[0]),
            None,
        )

    beside = [slopes_of(0), tokens(0), slopes_of(1), tokens(1)]
    hot_sum, token_grad = reduce_hot(hot_part, a, ns, beside)
    conv_weight_grad = unfold(place, hot_sum, stem, taps)
    return (token_grad, conv_weight_grad, pair_weight_grad)


def reduce_hot(x, a, ns, beside):
    steps = powers(ns)
    join = lax.optimization_barrier

    def swap(v, step):
        return lax.ppermute(v, "seq", xor_pairs(ns, step))

    keep, give = x
    x = keep + swap(give, steps[0]).astype(F32)
    done = None
    for at, step in enumerate(steps[1:]):
        size = x.shape[0] // 2
        bit = lax.rem(a // step, 2)
        keep = lax.dynamic_slice_in_dim(x, bit * size, size, 0)
        give = lax.dynamic_slice_in_dim(x, (1 - bit) * size, size, 0).astype(BF)
        keep, give, done = join((keep, give, done))
        got = swap(give, step)
        if at < len(beside):
            done = beside[at](done)
        keep, got, done = join((keep, got, done))
        x = keep + got.astype(F32)
    x = x.astype(BF)
    for at, step in enumerate(steps[:0:-1], len(steps) - 1):
        x, done = join((x, done))
        got = swap(x, step)
        if at < len(beside):
            done = beside[at](done)
        x, got, done = join((x, got, done))
        x = jnp.concatenate([x, got])
    return [x, swap(x, steps[0])], done[0]


def solution(mesh):
    placed = (
        P(None, "seq", None),
        P(None, "col"),
        P(None, "col", None),
        P("col"),
        P("col", None),
        P(),
        P(None, "seq", "col", None),
        P("seq", "col"),
    )
    return jax.shard_map(
        per_device,
        mesh=mesh,
        in_specs=placed,
        out_specs=(P(None, "seq", "col"), P(None, "col", None), P()),
        check_vma=False,
    )
```
